256 devices in a mesh: pb: 4 (over z_lo), vert: 64 (over z_hi, y, x, core).
Axes of the slice: x: 4, y: 4, z: 8 (z_hi: 2, z_lo: 4; z = z_hi * 4 + z_lo), core: 2. Of those that a mesh axis runs over, the one named last changes fastest.
Arguments:
- queries: float32 [8192, 768], P('pb'), may hold values from -16 to 16
- views: float32 [65536, 768], P(('vert', 'pb')), may hold values from -4 to 4
- positives: int32 [8192], P('pb'), may hold values from 0 to 65535
- query_weight: float32 [8192], P('pb'), may hold values from 0.3 to 3
- owners: int32 [65536], P('vert'), may hold values from 0 to 8191
- view_weight: float32 [65536], P('vert'), may hold values from 0.3 to 3
- view_kinds: int32 [65536], P('vert'), may hold values from 0 to 2
- kind_scale: float32 [3], replicated, may hold values from 2 to 8
Outputs:
- grad_q: float32 [8192, 768], P(('pb', 'vert'))
- grad_v: float32 [65536, 768], P(('vert', 'pb'))
- type_grad: float32 [3], replicated
The draws below stay inside these ranges and needn't reach their ends.
All inputs are finite; a program needn't handle non-finite values.
Results may differ from the reference program's by a relative error of at most 0.003.
The reference program's roundings to bfloat16 on the way count: a program that leaves them out, or rounds other values in their place, can miss the bound.
Values may be sent and summed in bfloat16 or wider, within the bound.
A program may use at most 64 MiB of HBM per device.

```python
import math
import jax
import jax.numpy as jnp
from jax import lax

D = 768
TYPES = 3
NQ = 8192
NV = 65536


def view_scales(key):
    spread = jax.random.uniform(jax.random.fold_in(key, 21), (NV,), jnp.float32, math.log(0.8), math.log(2.4))
    place = jnp.arange(NV, dtype=jnp.float32) / NV
    return jnp.exp(math.log(6.0) * place + spread)


def view_base(key):
    scales = view_scales(key)
    normal = jax.random.truncated_normal(jax.random.fold_in(key, 22), -4.0, 4.0, (NV, D), jnp.float32)
    return 0.02 * scales[:, None] * normal


def kind_values(key):
    return jax.random.randint(jax.random.fold_in(key, 23), (NV,), 0, TYPES, jnp.int32)


def scale_values(key):
    return jnp.exp(jax.random.uniform(jax.random.fold_in(key, 24), (TYPES,), jnp.float32, math.log(2.0), math.log(8.0)))


def draw_views(key, part):
    field = view_base(key)
    return field.astype(jnp.float32)


def draw_queries(key, part):
    key = jax.random.fold_in(key, 2)
    place = jnp.arange(NQ, dtype=jnp.float32) / NQ
    spread = jax.random.uniform(jax.random.fold_in(key, 3), (NQ,), jnp.float32, math.log(0.8), math.log(2.4))
    row_scale = jnp.exp(math.log(6.0) * place + spread)
    normal = jax.random.truncated_normal(jax.random.fold_in(key, 6), -4.0, 4.0, (NQ, D), jnp.float32)
    result = 0.02 * row_scale[:, None] * normal
    return result.astype(jnp.float32)


def draw_view_kinds(key, part):
    kinds = kind_values(key)
    return kinds


def draw_kind_scale(key, part):
    table = scale_values(key)
    return table.astype(jnp.float32)


def touch_ends(values, key, least, high):
    dims = values.shape
    spot = [jax.random.randint(jax.random.fold_in(key, axis), (), 0, dims[axis]) for axis in range(len(dims))]
    values = values.at[tuple(spot)].set(least)
    longest = dims.index(max(dims))
    spot[longest] = (spot[longest] + 1) % dims[longest]
    return values.at[tuple(spot)].set(high)


def levels(rng, dims, split, low, largest):
    gain, own = 1.0, jax.random.fold_in(rng, 6)
    for axis_at, parts in split:
        draws = jnp.exp(jax.random.uniform(jax.random.fold_in(own, axis_at), (parts,), jnp.float32, low / len(split), largest / len(split)))
        gain = gain * jnp.repeat(draws, dims[axis_at] // parts).reshape([-1 if axis == axis_at else 1 for axis in range(len(dims))])
    return gain


def setup_inputs(seed: int = 0) -> dict:
    keys = jax.random.split(jax.random.key(seed), 9)
    queries = draw_queries(jax.random.fold_in(keys[8], 71), 0)
    views = draw_views(jax.random.fold_in(keys[8], 71), 0)
    positives = touch_ends(jax.random.randint(keys[2], (NQ,), 0, NV), jax.random.fold_in(keys[2], 1), 0, NV - 1).astype(jnp.int32)
    query_weight = jnp.clip(jnp.exp(math.log(3.0) - 2.3025851 * jax.random.uniform(keys[3], (NQ,), jnp.float32) ** levels(keys[3], (NQ,), ((0, 4),), -0.2, 0.2)), 0.3, 3.0)
    owners = touch_ends(jax.random.randint(keys[4], (NV,), 0, NQ), jax.random.fold_in(keys[4], 1), 0, NQ - 1).astype(jnp.int32)
    view_weight = jnp.clip(jnp.exp(math.log(3.0) - 2.3025851 * jax.random.uniform(keys[5], (NV,), jnp.float32) ** levels(keys[5], (NV,), ((0, 64),), -0.2, 0.2)), 0.3, 3.0)
    view_kinds = draw_view_kinds(jax.random.fold_in(keys[8], 71), 0)
    kind_scale = draw_kind_scale(jax.random.fold_in(keys[8], 71), 0)
    return {"queries": queries, "views": views, "positives": positives, "query_weight": query_weight, "owners": owners, "view_weight": view_weight, "view_kinds": view_kinds, "kind_scale": kind_scale}


def reference(queries, views, positives, query_weight, owners, view_weight, view_kinds, kind_scale):
    q_half = queries.astype(jnp.bfloat16)
    v_half = views.astype(jnp.bfloat16)
    kind_ids = jnp.arange(TYPES, dtype=jnp.int32)
    kind_hot = (view_kinds[:, None] == kind_ids[None, :]).astype(jnp.float32)
    col_scale = jnp.sum(kind_hot * kind_scale[None, :], axis=1)
    block_rows = math.gcd(NQ, 512)
    block_count = NQ // block_rows
    q_blocks = q_half.reshape(block_count, block_rows, D)
    view_ids = jnp.arange(NV, dtype=jnp.int32)

    def scored(q_block):
        return jnp.dot(q_block, v_half.T, preferred_element_type=jnp.float32) * col_scale[None, :]

    def first_pass(running, q_block):
        col_peak, col_total = running
        scores = scored(q_block)
        row_peak = jnp.max(scores, axis=1)
        row_lse = row_peak + jnp.log(jnp.sum(jnp.exp(scores - row_peak[:, None]), axis=1))
        merged_max = jnp.maximum(col_peak, jnp.max(scores, axis=0))
        col_total = col_total * jnp.exp(col_peak - merged_max) + jnp.sum(jnp.exp(scores - merged_max[None, :]), axis=0)
        return (merged_max, col_total), row_lse

    initial = (jnp.full((NV,), -jnp.inf, jnp.float32), jnp.zeros((NV,), jnp.float32))
    (col_peak, col_total), row_lse = lax.scan(first_pass, initial, q_blocks)
    col_lse = col_peak + jnp.log(col_total)
    row_lse = row_lse.reshape(NQ)
    first_rows = jnp.arange(block_count, dtype=jnp.int32) * block_rows

    def second_pass(running, operands):
        grad_views, col_terms = running
        q_block, lse_block, weight_block, pos_block, first_row = operands
        scores = scored(q_block)
        pos_hot = (pos_block[:, None] == view_ids[None, :]).astype(jnp.float32)
        row_ids = first_row + jnp.arange(block_rows, dtype=jnp.int32)
        own_hot = (row_ids[:, None] == owners[None, :]).astype(jnp.float32)
        grad = weight_block[:, None] * (jnp.exp(scores - lse_block[:, None]) - pos_hot)
        grad = grad + view_weight[None, :] * (jnp.exp(scores - col_lse[None, :]) - own_hot)
        col_terms = col_terms + jnp.sum(grad * scores, axis=0)
        halfway = (grad * col_scale[None, :]).astype(jnp.bfloat16)
        grad_views = grad_views + jnp.dot(halfway.T, q_block, preferred_element_type=jnp.float32)
        grad_rows = jnp.dot(halfway, v_half, preferred_element_type=jnp.float32)
        return (grad_views, col_terms), grad_rows

    initial = (jnp.zeros((NV, D), jnp.float32), jnp.zeros((NV,), jnp.float32))
    operands = (q_blocks, row_lse.reshape(block_count, block_rows), query_weight.reshape(block_count, block_rows),
                positives.reshape(block_count, block_rows), first_rows)
    (grad_v, col_terms), grad_rows = lax.scan(second_pass, initial, operands)
    grad_q = grad_rows.reshape(NQ, D)
    type_grad = jnp.sum(kind_hot * col_terms[:, None], axis=0) / NQ
    return grad_q, grad_v, type_grad
```

```python
import functools
import math

import jax
import jax.numpy as jnp
from jax import lax
from jax.experimental import pallas as pl
from jax.experimental.pallas import tpu as pltpu
from jax.sharding import PartitionSpec as P

MESH = pl.DeviceIdType.MESH
LOG2E = math.log2(math.e)
LN2 = math.log(2.0)
NPB = 4
NX = 4
NY = 4
NA = 8
NB = 8
CHUNK = 256
F32 = jnp.float32
BF16 = jnp.bfloat16


def kernel(total_queries, kscale_ref, views_ref, q_hbm, pos_ref, qw_ref, own_ref, vw_ref, kind_ref,
           gq_out, gv_out, tg_out,
           qb, qt, vb, S, H, stat, arep, qwrep, posrep, gq, gvt, zs, zrl, zrr, crecv,
           sa1, sb1, ra1, rb1, sa2, sb2, ra2, rb2, acca, accb, zra, zrb,
           colst, rowa, rowb, colfin, rowfin, ta, tb, tp,
           qsem, ag_send, ag_recv, col_send, col_recv, row_send, row_recv, t_send, t_recv,
           c_send, c_recv, x_send, x_recv, z_send, zl_recv, zr_recv):
    p = lax.axis_index("pb")
    v = lax.axis_index("vert")
    core = v % 2
    x = (v // 2) % NX
    y = (v // (2 * NX)) % NY
    zh = v // (2 * NX * NY)
    a_me = v % NA
    b_me = v // NA
    rows, width = qb.shape
    nchunk = rows // CHUNK
    vcols = vb.shape[1]
    groups = nchunk * 4
    gpc = groups // nchunk

    def vert_of(zh_, y_, x_, c_):
        return ((zh_ * NY + y_) * NX + x_) * 2 + c_

    def remote(src, dst, ssem, rsem, dev):
        return pltpu.make_async_remote_copy(src_ref=src, dst_ref=dst, send_sem=ssem, recv_sem=rsem,
                                            device_id=dev, device_id_type=MESH)

    for r in range(nchunk):
        pltpu.make_async_copy(q_hbm.at[pl.ds(r * gpc, gpc)], gq.at[pl.ds(r * gpc, gpc)], qsem.at[r]).start()

    peers = [((p + d) % NPB, v) for d in range(1, NPB)]
    peers_a = [(p, b_me * NA + (a_me + d) % NA) for d in range(1, NA)]
    peers_b = [(p, ((b_me + d) % NB) * NA + a_me) for d in range(1, NB)]
    barrier = pltpu.get_barrier_semaphore()
    for dev in peers + peers_a + peers_b:
        pl.semaphore_signal(barrier, inc=1, device_id=dev, device_id_type=MESH)
    vb[p] = views_ref[...].astype(BF16)
    pl.semaphore_wait(barrier, len(peers) + len(peers_a) + len(peers_b))

    def send_right(k, s):
        return remote(vb.at[k], vb.at[k], ag_send.at[s], ag_recv.at[k], (p + 1, v))

    def send_left(k, s):
        return remote(vb.at[k], vb.at[k], ag_send.at[3 + s], ag_recv.at[k], (p - 1, v))

    def wait_views(k):
        remote(vb.at[k], vb.at[k], ag_send.at[0], ag_recv.at[k], (p, v)).wait_recv()

    @pl.when(p < NPB - 1)
    def _():
        send_right(p, 0).start()

    @pl.when(p > 0)
    def _():
        send_left(p, 0).start()

    def forward(k):
        @pl.when(jnp.logical_and(k < p, p < NPB - 1))
        def _():
            send_right(k, p - k).start()

        @pl.when(jnp.logical_and(k > p, p > 0))
        def _():
            send_left(k, k - p).start()

    side = p // 2
    near = p + side * (3 - 2 * p)
    base = [near, 1 - near, 2, 3]
    order = [b + side * (3 - 2 * b) for b in base]

    k0, k1, k2 = kscale_ref[0], kscale_ref[1], kscale_ref[2]

    def scale_of(k):
        kind = kind_ref[k]
        return jnp.where(kind == 0, k0, jnp.where(kind == 1, k1, k2))

    def cast_queries(r, carry):
        pltpu.make_async_copy(q_hbm.at[pl.ds(r * gpc, gpc)], gq.at[pl.ds(r * gpc, gpc)], qsem.at[r]).wait()
        block = gq[pl.ds(r * gpc, gpc)].reshape(CHUNK, width)
        at = pl.multiple_of(r * CHUNK, CHUNK)
        qb[pl.ds(at, CHUNK), :] = block.astype(BF16)
        qt[:, pl.ds(at, CHUNK)] = block.T.astype(BF16)
        return carry

    lax.fori_loop(0, nchunk, cast_queries, 0)

    def spread(r, carry):
        at = pl.multiple_of(r * 128, 128)
        qwrep[pl.ds(at, 128), :] = jnp.broadcast_to(qw_ref[pl.ds(r, 1), :], (128, 128)).T
        posrep[pl.ds(at, 128), :] = jnp.broadcast_to(pos_ref[pl.ds(r, 1), :], (128, 128)).T
        return carry

    lax.fori_loop(0, rows // 128, spread, 0)

    lane = lax.broadcasted_iota(jnp.int32, (CHUNK, 128), 1)

    def first_pass(t):
        k = order[t]
        scale = scale_of(k) * LOG2E

        def step(r, carry):
            peak, total = carry
            at = pl.multiple_of(r * CHUNK, CHUNK)
            s = lax.dot_general(qb[pl.ds(at, CHUNK), :], vb[k], (((1,), (1,)), ((), ())),
                                preferred_element_type=F32) * scale
            S[k, pl.ds(at, CHUNK), :] = s
            m = jnp.max(s, axis=1, keepdims=True)
            lse = m + jnp.log2(jnp.sum(jnp.exp2(s - m), axis=1, keepdims=True))
            if t == 0:
                stat[pl.ds(at, CHUNK), :] = jnp.broadcast_to(lse, (CHUNK, 128))
            else:
                stat[pl.ds(at, CHUNK), :] = jnp.where(lane == t, lse, stat[pl.ds(at, CHUNK), :])
            merged = jnp.maximum(peak, jnp.max(s, axis=0, keepdims=True))
            total = total * jnp.exp2(peak - merged) + jnp.sum(jnp.exp2(s - merged), axis=0, keepdims=True)
            return merged, total

        start = (jnp.full((1, vcols), -jnp.inf, F32), jnp.zeros((1, vcols), F32))
        peak, total = lax.fori_loop(0, nchunk, step, start)
        colst[p, k] = peak + jnp.log2(total)

    first_pass(0)
    for t in (1, 2):
        wait_views(order[t])
        forward(order[t])
    first_pass(1)
    first_pass(2)
    wait_views(order[3])
    forward(order[3])
    first_pass(3)

    sends = []

    def go(copy):
        copy.start()
        sends.append(copy)

    for d in range(1, NPB):
        go(remote(colst.at[p], colst.at[p], col_send.at[d], col_recv.at[p], ((p + d) % NPB, v)))

    def gather_rows(r, carry):
        at = pl.multiple_of(r * 128, 128)
        turned = stat[pl.ds(at, 128), :].T[0:NPB, :]
        m = jnp.max(turned, axis=0, keepdims=True)
        rowa[a_me, pl.ds(r, 1), :] = m + jnp.log2(jnp.sum(jnp.exp2(turned - m), axis=0, keepdims=True))
        return carry

    lax.fori_loop(0, rows // 128, gather_rows, 0)

    def log_sum(parts):
        m = parts[0]
        for part in parts[1:]:
            m = jnp.maximum(m, part)
        total = jnp.exp2(parts[0] - m)
        for part in parts[1:]:
            total = total + jnp.exp2(part - m)
        return m + jnp.log2(total)

    def exchange_a(buf, ssem, rsem, base_):
        for d in range(1, NA):
            go(remote(buf.at[a_me], buf.at[a_me], ssem.at[base_ + d], rsem.at[base_ + a_me], peers_a[d - 1]))

    def exchange_b(buf, ssem, rsem, base_):
        for d in range(1, NB):
            go(remote(buf.at[b_me], buf.at[b_me], ssem.at[base_ + d], rsem.at[base_ + b_me], peers_b[d - 1]))

    def collect(buf, ssem, rsem, base_, me, n):
        for d in range(1, n):
            src = (me + d) % n
            remote(buf.at[src], buf.at[src], ssem.at[base_ + d], rsem.at[base_ + src], (p, v)).wait_recv()

    exchange_a(rowa, row_send, row_recv, 0)
    collect(rowa, row_send, row_recv, 0, a_me, NA)
    rowb[b_me] = log_sum([rowa[i] for i in range(NA)])
    exchange_b(rowb, row_send, row_recv, NA)
    collect(colst, col_send, col_recv, 0, p, NPB)
    col_lse = [log_sum([colst[i, k] for i in range(NPB)]) for k in range(NPB)]
    for k in range(NPB):
        colfin[k] = col_lse[k] - jnp.log2(vw_ref[k])
    collect(rowb, row_send, row_recv, NA, b_me, NB)
    rowfin[...] = log_sum([rowb[i] for i in range(NB)]) - jnp.log2(qw_ref[...])

    def spread_lse(r, carry):
        at = pl.multiple_of(r * 128, 128)
        arep[pl.ds(at, 128), :] = jnp.broadcast_to(rowfin[pl.ds(r, 1), :], (128, 128)).T
        return carry

    lax.fori_loop(0, rows // 128, spread_lse, 0)

    lane_f = lax.broadcasted_iota(jnp.int32, (CHUNK, 128), 1).astype(F32)
    row_id = lax.broadcasted_iota(jnp.int32, (CHUNK, 128), 0)

    def second_pass(t):
        k = order[t]
        scale = scale_of(k)
        shift = colfin[k]
        weight = vw_ref[k]
        owner = own_ref[k] - p * rows

        def step(r, carry):
            at = pl.multiple_of(r * CHUNK, CHUNK)
            ra, rw, rp = arep[pl.ds(at, CHUNK), :], qwrep[pl.ds(at, CHUNK), :], posrep[pl.ds(at, CHUNK), :]
            out = []
            for h in range(vcols // 128):
                part = slice(h * 128, (h + 1) * 128)
                s = S[k, pl.ds(at, CHUNK), part]
                g = jnp.exp2(s - ra) + jnp.exp2(s - shift[:, part])
                col = lane_f + (k * vcols + h * 128).astype(F32)
                g = g - jnp.where(rp == col, rw, 0.0)
                g = g - jnp.where(row_id == owner[:, part] - at, weight[:, part], 0.0)
                H[k, pl.ds(at, CHUNK), part] = (g * scale[:, part]).astype(BF16)
                out.append(carry[h] + jnp.sum(g * s, axis=0, keepdims=True))
            return tuple(out)

        zero = jnp.zeros((1, 128), F32)
        terms = lax.fori_loop(0, nchunk, step, (zero,) * (vcols // 128))
        kind = kind_ref[k]
        kinds = []
        for t_ in range(3):
            kinds.append(sum(jnp.where(kind[:, h * 128:(h + 1) * 128] == t_, terms[h], 0.0)
                             for h in range(vcols // 128)))

        def grad_views(i, carry):
            at = pl.multiple_of(i * CHUNK, CHUNK)
            gvt[k, pl.ds(at, CHUNK), :] = jnp.dot(qt[pl.ds(at, CHUNK), :], H[k], preferred_element_type=F32)
            return carry

        lax.fori_loop(0, width // CHUNK, grad_views, 0)
        return kinds

    def right(k):
        return remote(zs.at[k], zrl.at[k], z_send.at[k], zl_recv.at[k], (p + 1, v))

    def left(k):
        return remote(zs.at[k], zrr.at[k], z_send.at[k], zr_recv.at[k], (p - 1, v))

    kinds = [jnp.zeros((1, 128), F32)] * 3
    for t in (3, 2, 1, 0):
        more = second_pass(t)
        kinds = [a + b for a, b in zip(kinds, more)]
        if t > 0:
            k = order[t]

            @pl.when(p == 0)
            def _():
                zs[k] = gvt[k].astype(BF16)
                right(k).start()

            @pl.when(p == NPB - 1)
            def _():
                zs[k] = gvt[k].astype(BF16)
                left(k).start()

    ta[a_me] = jnp.concatenate(kinds + [jnp.zeros((5, 128), F32)], axis=0) * (LN2 / total_queries)
    exchange_a(ta, t_send, t_recv, 0)

    def relay_right(k):
        right(k).wait_recv()
        zs[k] = (gvt[k] + zrl[k].astype(F32)).astype(BF16)
        right(k).start()

    def relay_left(k):
        left(k).wait_recv()
        zs[k] = (gvt[k] + zrr[k].astype(F32)).astype(BF16)
        left(k).start()

    @pl.when(p == 1)
    def _():
        relay_right(3)

    @pl.when(p == 2)
    def _():
        relay_left(0)

    other = vert_of(zh, y, x, 1 - core)

    def core_copy(r):
        return remote(gq.at[pl.ds(r * gpc, gpc), 1 - core], crecv.at[pl.ds(r * gpc, gpc)],
                      c_send.at[r], c_recv.at[r], (p, other))

    def grad_queries(r, carry):
        at = pl.multiple_of(r * CHUNK, CHUNK)
        acc = jnp.dot(H[0, pl.ds(at, CHUNK), :], vb[0], preferred_element_type=F32)
        for k in range(1, NPB):
            acc = acc + jnp.dot(H[k, pl.ds(at, CHUNK), :], vb[k], preferred_element_type=F32)
        gq[pl.ds(r * gpc, gpc)] = acc.reshape(gpc, 2, CHUNK // (2 * gpc), width)
        core_copy(r).start()
        return carry

    lax.fori_loop(0, nchunk, grad_queries, 0)

    half = width // 2
    for r in range(nchunk):
        core_copy(r).wait_recv()
        for g in range(r * gpc, (r + 1) * gpc):
            gz, gy, gx = g // (NX * NY), (g // NX) % NY, g % NX
            val = gq[g, core] + crecv[g]
            crecv[g] = val
            sa1[gx, gz * NY + gy] = val[:, :half].astype(BF16)
            sb1[gy, gz * NX + gx] = val[:, half:].astype(BF16)

    def to_x(src, dst, at, d):
        return remote(src, dst, x_send.at[at + d], x_recv.at[at + x], (p, vert_of(zh, y, (x + d) % NX, core)))

    def to_y(src, dst, at, d):
        return remote(src, dst, x_send.at[at + d], x_recv.at[at + y], (p, vert_of(zh, (y + d) % NY, x, core)))

    for d in range(1, 4):
        go(to_x(sa1.at[(x + d) % NX], ra1.at[x], 0, d))
        go(to_y(sb1.at[(y + d) % NY], rb1.at[y], 4, d))

    collect(ta, t_send, t_recv, 0, a_me, NA)
    tb[b_me] = sum(ta[i] for i in range(NA))
    exchange_b(tb, t_send, t_recv, NA)

    @pl.when(p == 1)
    def _():
        relay_right(2)
        relay_left(0)

    @pl.when(p == 2)
    def _():
        relay_left(1)
        relay_right(3)

    collect(tb, t_send, t_recv, NA, b_me, NB)
    tp[p] = sum(tb[i] for i in range(NB))
    for d in range(1, NPB):
        go(remote(tp.at[p], tp.at[p], t_send.at[NA + NB + d], t_recv.at[NA + NB + p], ((p + d) % NPB, v)))

    collect(ra1, x_send, x_recv, 0, x, NX)
    for gz in range(2):
        for gy in range(NY):
            i = gz * NY + gy
            val = crecv[i * NX + x][:, :half]
            for d in range(1, NX):
                val = val + ra1[(x + d) % NX, i].astype(F32)
            acca[i] = val
            sa2[gy, gz] = val.astype(BF16)
    for d in range(1, 4):
        go(to_y(sa2.at[(y + d) % NY], ra2.at[y], 8, d))

    collect(rb1, x_send, x_recv, 4, y, NY)
    for gz in range(2):
        for gx in range(NX):
            i = gz * NX + gx
            val = crecv[gz * (NX * NY) + y * NX + gx][:, half:]
            for d in range(1, NY):
                val = val + rb1[(y + d) % NY, i].astype(F32)
            accb[i] = val
            sb2[gx, gz] = val.astype(BF16)
    for d in range(1, 4):
        go(to_x(sb2.at[(x + d) % NX], rb2.at[x], 12, d))

    collect(ra2, x_send, x_recv, 8, y, NY)
    for gz in range(2):
        val = acca[gz * NY + y]
        for d in range(1, NY):
            val = val + ra2[(y + d) % NY, gz].astype(F32)
        acca[gz * NY + y] = val
    far = (p, vert_of(1 - zh, y, x, core))
    last_a = remote(acca.at[(1 - zh) * NY + y], zra, x_send.at[16], x_recv.at[16], far)
    last_a.start()

    collect(rb2, x_send, x_recv, 12, x, NX)
    for gz in range(2):
        val = accb[gz * NX + x]
        for d in range(1, NX):
            val = val + rb2[(x + d) % NX, gz].astype(F32)
        accb[gz * NX + x] = val
    last_b = remote(accb.at[(1 - zh) * NX + x], zrb, x_send.at[17], x_recv.at[17], far)
    last_b.start()

    for d in range(1, NPB):
        src = (p + d) % NPB
        remote(tp.at[src], tp.at[src], t_send.at[0], t_recv.at[NA + NB + src], (p, v)).wait_recv()
    sums = sum(tp[i] for i in range(NPB))
    tg_out[...] = jnp.broadcast_to(jnp.sum(sums, axis=1, keepdims=True), sums.shape)

    last_a.wait_recv()
    gq_out[:, :half] = acca[zh * NY + y] + zra[...]
    last_b.wait_recv()
    gq_out[:, half:] = accb[zh * NX + x] + zrb[...]

    @pl.when(p > 0)
    def _():
        right(p).wait_recv()
        gvt[p] = gvt[p] + zrl[p].astype(F32)

    @pl.when(p < NPB - 1)
    def _():
        left(p).wait_recv()
        gvt[p] = gvt[p] + zrr[p].astype(F32)

    gv_out[...] = gvt[p].T

    last_a.wait_send()
    last_b.wait_send()
    for copy in sends:
        copy.wait_send()
    for r in range(nchunk):
        core_copy(r).wait_send()
    for k in range(NPB):
        @pl.when(k != p)
        def _():
            right(k).wait_send()
    for s in range(NPB - 1):
        @pl.when(jnp.logical_and(p < NPB - 1, s <= p))
        def _():
            send_right(p, s).wait_send()

        @pl.when(jnp.logical_and(p > 0, s <= NPB - 1 - p))
        def _():
            send_left(p, s).wait_send()


def on_device(queries, views, positives, query_weight, owners, view_weight, view_kinds, kind_scale):
    rows, width = queries.shape
    vcols = views.shape[0]
    tile_cols = NPB * vcols
    nchunk = rows // CHUNK
    groups = 4 * nchunk
    sub = rows // (2 * groups)
    half = width // 2
    col_anchor = lax.axis_index("vert") * tile_cols
    pos = (positives - col_anchor).astype(F32).reshape(rows // 128, 128)
    qw = query_weight.reshape(rows // 128, 128)
    own = owners.reshape(NPB, 1, vcols)
    vw = view_weight.reshape(NPB, 1, vcols)
    kind = view_kinds.reshape(NPB, 1, vcols)
    vmem = pl.BlockSpec(memory_space=pltpu.VMEM)
    V = pltpu.VMEM
    dma = pltpu.SemaphoreType.DMA
    gq, gv, tg = pl.pallas_call(
        functools.partial(kernel, rows * NPB),
        out_shape=(
            jax.ShapeDtypeStruct((sub, width), F32),
            jax.ShapeDtypeStruct((vcols, width), F32),
            jax.ShapeDtypeStruct((8, 128), F32),
        ),
        in_specs=[pl.BlockSpec(memory_space=pltpu.SMEM), vmem, pl.BlockSpec(memory_space=pl.ANY)] + [vmem] * 5,
        out_specs=(vmem, vmem, vmem),
        scratch_shapes=[
            V((rows, width), BF16),
            V((width, rows), BF16),
            V((NPB, vcols, width), BF16),
            V((NPB, rows, vcols), F32),
            V((NPB, rows, vcols), BF16),
            V((rows, 128), F32),
            V((rows, 128), F32),
            V((rows, 128), F32),
            V((rows, 128), F32),
            V((groups, 2, sub, width), F32),
            V((NPB, width, vcols), F32),
            V((NPB, width, vcols), BF16),
            V((NPB, width, vcols), BF16),
            V((NPB, width, vcols), BF16),
            V((groups, sub, width), F32),
            V((NX, 8, sub, half), BF16),
            V((NY, 8, sub, half), BF16),
            V((NX, 8, sub, half), BF16),
            V((NY, 8, sub, half), BF16),
            V((NY, 2, sub, half), BF16),
            V((NX, 2, sub, half), BF16),
            V((NY, 2, sub, half), BF16),
            V((NX, 2, sub, half), BF16),
            V((8, sub, half), F32),
            V((8, sub, half), F32),
            V((sub, half), F32),
            V((sub, half), F32),
            V((NPB, NPB, 1, vcols), F32),
            V((NA, rows // 128, 128), F32),
            V((NB, rows // 128, 128), F32),
            V((NPB, 1, vcols), F32),
            V((rows // 128, 128), F32),
            V((NA, 8, 128), F32),
            V((NB, 8, 128), F32),
            V((NPB, 8, 128), F32),
            dma((nchunk,)),
            dma((6,)), dma((NPB,)),
            dma((NPB,)), dma((NPB,)),
            dma((NA + NB,)), dma((NA + NB,)),
            dma((NA + NB + NPB,)), dma((NA + NB + NPB,)),
            dma((nchunk,)), dma((nchunk,)),
            dma((18,)), dma((18,)),
            dma((NPB,)), dma((NPB,)), dma((NPB,)),
        ],
        compiler_params=pltpu.CompilerParams(collective_id=0, has_side_effects=True,
                                             vmem_limit_bytes=62 * 1024 * 1024),
    )(kind_scale, views, queries.reshape(groups, 2, sub, width), pos, qw, own, vw, kind)
    return gq, gv, tg[:3, 0]


def solution(mesh):
    in_specs = (P("pb", None), P(("vert", "pb"), None), P("pb"), P("pb"), P("vert"), P("vert"), P("vert"), P())
    out_specs = (P(("pb", "vert"), None), P(("vert", "pb"), None), P())
    return jax.shard_map(on_device, mesh=mesh, in_specs=in_specs, out_specs=out_specs, check_vma=False)
```

```python
import functools
import math

import jax
import jax.numpy as jnp
from jax import lax
from jax.experimental import pallas as pl
from jax.experimental.pallas import tpu as pltpu
from jax.sharding import PartitionSpec as P

MESH = pl.DeviceIdType.MESH
LOG2E = math.log2(math.e)
LN2 = math.log(2.0)
NPB = 4
NX = 4
NY = 4
NA = 8
NB = 16
CHUNK = 256
F32 = jnp.float32
BF16 = jnp.bfloat16


def kernel(total_queries, kscale_ref, views_ref, q_hbm, pos_ref, qw_ref, own_ref, vw_ref, kind_ref,
           gq_out, gv_out, tg_out,
           qb, qt, qf, vb, S, H, qslice, qzs, pq, pqf, rep, qwrep, posrep, gown, csend, crecv,
           sa1, sb1, ra1, rb1, sa2, sb2, ra2, rb2, acca, accb, res, zres, gvt, zs, zr,
           colpart, rowpart, colx, colfin, rowa, rowb, rowfin, ta, tb, tp,
           qsem, slsem, ag_send, ag_recv, core_send, core_recv, vz_send, vz_recv,
           col_send, col_recv, row_send, row_recv, t_send, t_recv,
           c_send, c_recv, x_send, x_recv, z_send, z_recv):
    p = lax.axis_index("pb")
    v = lax.axis_index("vert")
    core = v % 2
    x = (v // 2) % NX
    y = (v // (2 * NX)) % NY
    zh = v // (2 * NX * NY)
    even = p % 2
    upper = p // 2
    mate = p + 1 - 2 * even
    far = (p + 2) % NPB
    a_me = v % NA
    b_me = (upper * 2 + zh) * NY + y
    rows, width = qb.shape
    nchunk = rows // CHUNK
    vcols = views_ref.shape[0]
    half = width // 2
    sub = gown.shape[3]

    def vert_of(zh_, y_, x_, c_):
        return ((zh_ * NY + y_) * NX + x_) * 2 + c_

    def remote(src, dst, ssem, rsem, dev):
        return pltpu.make_async_remote_copy(src_ref=src, dst_ref=dst, send_sem=ssem, recv_sem=rsem,
                                            device_id=dev, device_id_type=MESH)

    here = (p, v)
    sends = []

    def go(copy):
        copy.start()
        sends.append(copy)

    sl_a = (y * NX + x) * 2 + core
    sl_b = 8 * NY + (x * NY + y) * 2 + core
    slices = []
    for i, sl in enumerate((sl_a, sl_b)):
        slices.append(pltpu.make_async_copy(q_hbm.at[sl // 16, (sl // 4) % 4, sl % 4], qslice.at[i], slsem.at[i]))
        slices[-1].start()

    def load(r):
        part = (r // 2, pl.ds((r % 2) * 2, 2))
        return pltpu.make_async_copy(q_hbm.at[part], gown.at[part], qsem.at[r])

    for r in range(nchunk):
        load(r).start()

    peers_a = [(p, (v // NA) * NA + (a_me + d) % NA) for d in range(1, NA)]
    peers_b = []
    for d in range(1, NB):
        i = (b_me + d) % NB
        peers_b.append(((i // 8) * 2 + even, vert_of((i // NY) % 2, i % NY, x, core)))
    peers = peers_a + peers_b + [(mate, v)]
    barrier = pltpu.get_barrier_semaphore()
    for dev in peers:
        pl.semaphore_signal(barrier, inc=1, device_id=dev, device_id_type=MESH)
    vb[0:vcols, :] = views_ref[...].astype(BF16)
    nrow = rows // 128
    pq[0:nrow, :] = pos_ref[...].astype(F32)
    pq[nrow:2 * nrow, :] = qw_ref[...]
    for i in range(2):
        slices[i].wait()
        qzs[i] = qslice[i].astype(BF16)
    pl.semaphore_wait(barrier, len(peers))

    def to_far(i, src, dst):
        return remote(src, dst, vz_send.at[i], vz_recv.at[i], (far, v))

    go(to_far(0, qzs.at[0], qf.at[0, y, x, core]))
    go(to_far(1, qzs.at[1], qf.at[1, x, y, core]))
    views_copy = remote(vb.at[pl.ds(0, vcols)], vb.at[pl.ds(vcols, vcols)], vz_send.at[2], vz_recv.at[2], (mate, v))
    go(views_copy)
    go(to_far(3, pq, pqf))

    def to_x(d):
        return (p, vert_of(zh, y, (x + d) % NX, core))

    def to_y(d):
        return (p, vert_of(zh, (y + d) % NY, x, core))

    twin = (p, vert_of(zh, y, x, 1 - core))

    k0, k1, k2 = kscale_ref[0], kscale_ref[1], kscale_ref[2]
    blocks = (p, mate)

    def scale_of(k):
        kind = kind_ref[k]
        return jnp.where(kind == 0, k0, jnp.where(kind == 1, k1, k2))

    scales = [scale_of(k) for k in blocks]
    scales2 = [s * LOG2E for s in scales]

    def cast_queries(r, carry):
        load(r).wait()
        block = gown[r // 2, pl.ds((r % 2) * 2, 2)].reshape(CHUNK, width)
        at = pl.multiple_of(r * CHUNK, CHUNK)
        qb[pl.ds(at, CHUNK), :] = block.astype(BF16)
        qt[:, pl.ds(at, CHUNK)] = block.T.astype(BF16)
        return carry

    lax.fori_loop(0, nchunk, cast_queries, 0)

    def score(q, at, ch, slots, row_at):
        tiles = []
        for sl in slots:
            cols = slice(sl * vcols, (sl + 1) * vcols)
            s = lax.dot_general(q, vb[cols, :], (((1,), (1,)), ((), ())),
                                preferred_element_type=F32) * scales2[sl]
            S[pl.ds(at, CHUNK), cols] = s
            peak = jnp.max(s, axis=0, keepdims=True)
            colpart[sl, pl.ds(ch, 1), :] = peak + jnp.log2(jnp.sum(jnp.exp2(s - peak), axis=0, keepdims=True))
            tiles += [s[:, h * 128:(h + 1) * 128] for h in range(vcols // 128)]
        m = functools.reduce(jnp.maximum, tiles)
        total = functools.reduce(jnp.add, [jnp.exp2(t - m) for t in tiles])
        for i in range(CHUNK // 128):
            mt = m[i * 128:(i + 1) * 128, :].T
            lt = total[i * 128:(i + 1) * 128, :].T
            peak = jnp.max(mt, axis=0, keepdims=True)
            lse = peak + jnp.log2(jnp.sum(lt * jnp.exp2(mt - peak), axis=0, keepdims=True))
            rowpart[row_at[0], pl.ds(row_at[1] * 2 + i, 1), :] = lse

    def own_pass(sl, first, last):
        def step(i, carry):
            for j in range(2):
                r = i * 2 + j
                at = pl.multiple_of(r * CHUNK, CHUNK)
                score(qb[pl.ds(at, CHUNK), :], at, r, (sl,), (sl, r))
            return carry

        lax.fori_loop(first // 2, last // 2, step, 0)

    def far_pass(parts):
        for h, o in parts:
            r = h * 4 + o
            q = qf[h, o].reshape(CHUNK, width)
            at = pl.multiple_of(rows + r * CHUNK, CHUNK)
            score(q, at, r + nchunk, (0, 1), (2, r))
            qt[:, pl.ds(at, CHUNK)] = q.T

    def got(ref, sem):
        remote(ref, ref, sem, sem, here).wait_recv()

    got(qf.at[0, y, x, core], vz_recv.at[0])
    for d in (1, 3, 2):
        go(remote(qf.at[0, y, x, core], qf.at[0, y, x, core], ag_send.at[d], ag_recv.at[x], to_x(d)))
    got(qf.at[1, x, y, core], vz_recv.at[1])
    for d in (1, 3, 2):
        go(remote(qf.at[1, x, y, core], qf.at[1, x, y, core], ag_send.at[4 + d], ag_recv.at[4 + y], to_y(d)))

    own_pass(0, 0, 4)

    for d in (1, 3, 2):
        got(qf.at[0, y, (x + d) % NX, core], ag_recv.at[(x + d) % NX])
    for d in (1, 3, 2):
        go(remote(qf.at[0, y, :, core], qf.at[0, y, :, core], ag_send.at[8 + d], ag_recv.at[8 + y], to_y(d)))
    for d in (1, 3, 2):
        got(qf.at[1, x, (y + d) % NY, core], ag_recv.at[4 + (y + d) % NY])
    for d in (1, 3, 2):
        go(remote(qf.at[1, x, :, core], qf.at[1, x, :, core], ag_send.at[12 + d], ag_recv.at[12 + x], to_x(d)))

    def to_twin(h, o):
        part = qf.at[h, o, :, core]
        go(remote(part, part, core_send.at[h * 4 + o], core_recv.at[h * 4 + o], twin))

    def from_twin(h, o):
        got(qf.at[h, o, :, 1 - core], core_recv.at[h * 4 + o])

    to_twin(0, y)
    to_twin(1, x)

    own_pass(0, 4, 8)

    def spread(src, first, dst, at0):
        def step(r, carry):
            at = pl.multiple_of(at0 + r * 128, 128)
            dst[pl.ds(at, 128), :] = jnp.broadcast_to(src[pl.ds(first + r, 1), :], (128, 128)).T
            return carry

        lax.fori_loop(0, nrow, step, 0)

    spread(pq, 0, posrep, 0)
    spread(pq, nrow, qwrep, 0)
    got(vb.at[pl.ds(vcols, vcols)], vz_recv.at[2])
    own_pass(1, 0, 8)
    got(pqf, vz_recv.at[3])
    spread(pqf, 0, posrep, rows)
    spread(pqf, nrow, qwrep, rows)

    from_twin(0, y)
    from_twin(1, x)
    far_pass([(0, y), (1, x)])
    for d in (1, 3):
        got(qf.at[0, (y + d) % NY, :, core], ag_recv.at[8 + (y + d) % NY])
        to_twin(0, (y + d) % NY)
        got(qf.at[1, (x + d) % NX, :, core], ag_recv.at[12 + (x + d) % NX])
        to_twin(1, (x + d) % NX)
    for d in (1, 3):
        from_twin(0, (y + d) % NY)
        from_twin(1, (x + d) % NX)
        far_pass([(0, (y + d) % NY), (1, (x + d) % NX)])
    got(qf.at[0, (y + 2) % NY, :, core], ag_recv.at[8 + (y + 2) % NY])
    to_twin(0, (y + 2) % NY)
    got(qf.at[1, (x + 2) % NX, :, core], ag_recv.at[12 + (x + 2) % NX])
    to_twin(1, (x + 2) % NX)
    from_twin(0, (y + 2) % NY)
    from_twin(1, (x + 2) % NX)
    far_pass([(0, (y + 2) % NY), (1, (x + 2) % NX)])

    def log_sum(parts):
        m = functools.reduce(jnp.maximum, parts)
        return m + jnp.log2(functools.reduce(jnp.add, [jnp.exp2(t - m) for t in parts]))

    def exchange_a(buf, ssem, rsem, base):
        for d in range(1, NA):
            go(remote(buf.at[a_me], buf.at[a_me], ssem.at[base + d], rsem.at[base + a_me], peers_a[d - 1]))

    def exchange_b(buf, ssem, rsem, base):
        for d in range(1, NB):
            go(remote(buf.at[b_me], buf.at[b_me], ssem.at[base + d], rsem.at[base + b_me], peers_b[d - 1]))

    def collect(buf, rsem, base, me, n):
        for d in range(1, n):
            src = (me + d) % n
            got(buf.at[src], rsem.at[base + src])

    rowa[a_me, upper] = log_sum([rowpart[0], rowpart[1]])
    rowa[a_me, 1 - upper] = rowpart[2]
    exchange_a(rowa, row_send, row_recv, 0)
    for sl in range(2):
        part = colpart[sl]
        m = jnp.max(part, axis=0, keepdims=True)
        at = even if sl == 0 else 1 - even
        colx[even, at] = m + jnp.log2(jnp.sum(jnp.exp2(part - m), axis=0, keepdims=True))
    go(remote(colx.at[even], colx.at[even], col_send.at[0], col_recv.at[0], (mate, v)))
    collect(rowa, row_recv, 0, a_me, NA)
    rowb[b_me] = log_sum([rowa[i] for i in range(NA)])
    exchange_b(rowb, row_send, row_recv, NA)
    got(colx.at[1 - even], col_recv.at[0])
    for sl in range(2):
        at = even if sl == 0 else 1 - even
        colfin[sl] = log_sum([colx[0, at], colx[1, at]]) - jnp.log2(vw_ref[blocks[sl]])
    collect(rowb, row_recv, NA, b_me, NB)
    row_lse = log_sum([rowb[i] for i in range(NB)])
    rowfin[...] = row_lse
    pqw = (pq, pqf)
    for b in range(2):
        at = upper if b == 0 else 1 - upper
        rowpart[b] = rowfin[at] - jnp.log2(pqw[b][nrow:2 * nrow, :])

    def spread_lse(b):
        def step(i, carry):
            for j in range(2):
                r = i * 2 + j
                at = pl.multiple_of(b * rows + r * 128, 128)
                rep[pl.ds(at, 128), :] = jnp.broadcast_to(rowpart[b, pl.ds(r, 1), :], (128, 128)).T
            return carry

        lax.fori_loop(0, nrow // 2, step, 0)

    spread_lse(1)

    lane = lax.broadcasted_iota(jnp.int32, (CHUNK, 128), 1).astype(F32)
    row_id = lax.broadcasted_iota(jnp.int32, (CHUNK, 128), 0)
    ntile = 2 * vcols // 128
    per = vcols // 128

    def tile(arr, h):
        return arr[h // per][:, (h % per) * 128:(h % per + 1) * 128]

    weights = [vw_ref[k] for k in blocks]
    owners = [own_ref[k] for k in blocks]
    shifts = [colfin[0], colfin[1]]
    col0 = [(v * (NPB * vcols) + k * vcols).astype(F32) for k in blocks]
    rounds = [(1, 1 - zh), (1, zh), (0, 1 - zh), (0, zh)]

    def core_copy(rd, o):
        return remote(csend.at[rd, o], crecv.at[rd, o], c_send.at[rd * 4 + o], c_recv.at[rd * 4 + o], twin)

    def grad_step(rd, o, terms):
        b, z = rounds[rd]
        at = pl.multiple_of(b * rows + z * (rows // 2) + o * CHUNK, CHUNK)
        first_row = (p if b == 0 else far) * rows + z * (rows // 2) + o * CHUNK
        ra, rw, rp = rep[pl.ds(at, CHUNK), :], qwrep[pl.ds(at, CHUNK), :], posrep[pl.ds(at, CHUNK), :]
        out, pieces = [], []
        for h in range(ntile):
            s = S[pl.ds(at, CHUNK), h * 128:(h + 1) * 128]
            g = jnp.exp2(s - ra) + jnp.exp2(s - tile(shifts, h))
            col = lane + (col0[h // per] + (h % per) * 128)
            g = g - jnp.where(rp == col, rw, 0.0)
            g = g - jnp.where(row_id == tile(owners, h) - first_row, tile(weights, h), 0.0)
            pieces.append((g * tile(scales, h)).astype(BF16))
            out.append(terms[h] + jnp.sum(g * s, axis=0, keepdims=True))
        hh = jnp.concatenate(pieces, axis=1)
        H[pl.ds(at, CHUNK), :] = hh
        acc = jnp.dot(hh, vb[...], preferred_element_type=F32).reshape(NX, 2, sub, width)
        first, second = acc[:, 0], acc[:, 1]
        gown[rd, o] = jnp.where(core == 0, first, second)
        csend[rd, o] = jnp.where(core == 0, second, first).astype(BF16)
        core_copy(rd, o).start()
        return tuple(out)

    def grad_half(rd, part, terms):
        for j in range(2):
            terms = grad_step(rd, part * 2 + j, terms)
        return terms

    def fold_core(rd):
        def step(o, carry):
            core_copy(rd, o).wait_recv()
            for i in range(NX):
                val = gown[rd, o, i] + crecv[rd, o, i].astype(F32)
                gown[rd, o, i] = val
                sa1[rd, i, o] = val[:, :half].astype(BF16)
                sb1[rd, o, i] = val[:, half:].astype(BF16)
            return carry

        lax.fori_loop(0, NY, step, 0)
        for d in (1, 3, 2):
            go(remote(sa1.at[rd, (x + d) % NX], ra1.at[rd, x], x_send.at[rd * 16 + d], x_recv.at[rd * 16 + x], to_x(d)))
            go(remote(sb1.at[rd, (y + d) % NY], rb1.at[rd, y], x_send.at[rd * 16 + 4 + d], x_recv.at[rd * 16 + 4 + y],
                      to_y(d)))

    def fold_first(rd):
        for d in (1, 3, 2):
            got(ra1.at[rd, (x + d) % NX], x_recv.at[rd * 16 + (x + d) % NX])
        for o in range(NY):
            val = gown[rd, o, x][:, :half]
            for d in range(1, NX):
                val = val + ra1[rd, (x + d) % NX, o].astype(F32)
            acca[rd, o] = val
            sa2[rd, o] = val.astype(BF16)
        for d in (1, 3, 2):
            go(remote(sa2.at[rd, (y + d) % NY], ra2.at[rd, y], x_send.at[rd * 16 + 8 + d], x_recv.at[rd * 16 + 8 + y],
                      to_y(d)))
        for d in (1, 3, 2):
            got(rb1.at[rd, (y + d) % NY], x_recv.at[rd * 16 + 4 + (y + d) % NY])
        for i in range(NX):
            val = gown[rd, y, i][:, half:]
            for d in range(1, NY):
                val = val + rb1[rd, (y + d) % NY, i].astype(F32)
            accb[rd, i] = val
            sb2[rd, i] = val.astype(BF16)
        for d in (1, 3, 2):
            go(remote(sb2.at[rd, (x + d) % NX], rb2.at[rd, x], x_send.at[rd * 16 + 12 + d],
                      x_recv.at[rd * 16 + 12 + x], to_x(d)))

    def fold_second(rd):
        for d in (1, 3, 2):
            got(ra2.at[rd, (y + d) % NY], x_recv.at[rd * 16 + 8 + (y + d) % NY])
        val = acca[rd, y]
        for d in range(1, NY):
            val = val + ra2[rd, (y + d) % NY].astype(F32)
        res[rd, :, :half] = val
        for d in (1, 3, 2):
            got(rb2.at[rd, (x + d) % NX], x_recv.at[rd * 16 + 12 + (x + d) % NX])
        val = accb[rd, x]
        for d in range(1, NX):
            val = val + rb2[rd, (x + d) % NX].astype(F32)
        res[rd, :, half:] = val
        if rd < 3:
            b, z = rounds[rd]
            go(remote(res.at[rd], zres.at[rd], z_send.at[rd], z_recv.at[rd], (p if b == 0 else far, vert_of(z, y, x, core))))

    def grad_views(sl):
        def step(i, carry):
            at = pl.multiple_of(i * CHUNK, CHUNK)
            gvt[sl, pl.ds(at, CHUNK), :] = jnp.dot(qt[pl.ds(at, CHUNK), :], H[:, sl * vcols:(sl + 1) * vcols],
                                                   preferred_element_type=F32)
            return carry

        lax.fori_loop(0, width // CHUNK, step, 0)

    terms = (jnp.zeros((1, 128), F32),) * ntile
    terms = grad_half(0, 0, terms)
    terms = grad_half(0, 1, terms)
    spread_lse(0)
    fold_core(0)
    terms = grad_half(1, 0, terms)
    terms = grad_half(1, 1, terms)
    terms = grad_half(2, 0, terms)
    fold_core(1)
    terms = grad_half(2, 1, terms)
    fold_first(0)
    terms = grad_half(3, 0, terms)
    fold_core(2)
    terms = grad_half(3, 1, terms)
    grad_views(1)
    zs[...] = gvt[1].astype(BF16)
    go(remote(zs, zr, z_send.at[3], z_recv.at[3], (mate, v)))
    fold_core(3)

    kinds = []
    for t in range(3):
        kinds.append(functools.reduce(jnp.add, [
            jnp.where(tile([kind_ref[k] for k in blocks], h) == t, terms[h], 0.0) for h in range(ntile)]))
    ta[a_me] = jnp.concatenate(kinds + [jnp.zeros((5, 128), F32)], axis=0) * (LN2 / total_queries)
    exchange_a(ta, t_send, t_recv, 0)

    fold_first(1)
    grad_views(0)
    fold_second(0)
    collect(ta, t_recv, 0, a_me, NA)
    tb[b_me] = functools.reduce(jnp.add, [ta[i] for i in range(NA)])
    exchange_b(tb, t_send, t_recv, NA)
    fold_first(2)
    fold_second(1)
    collect(tb, t_recv, NA, b_me, NB)
    tp[even] = functools.reduce(jnp.add, [tb[i] for i in range(NB)])
    go(remote(tp.at[even], tp.at[even], t_send.at[NA + NB], t_recv.at[NA + NB], (mate, v)))
    fold_first(3)
    fold_second(2)
    got(zr, z_recv.at[3])
    gv_out[...] = (gvt[0] + zr[...].astype(F32)).T
    got(tp.at[1 - even], t_recv.at[NA + NB])
    sums = tp[0] + tp[1]
    tg_out[...] = jnp.broadcast_to(jnp.sum(sums, axis=1, keepdims=True), sums.shape)
    fold_second(3)
    total = res[3]
    for i in range(3):
        got(zres.at[i], z_recv.at[i])
        total = total + zres[i]
    gq_out[...] = total

    for copy in sends:
        copy.wait_send()
    for rd in range(4):
        for o in range(4):
            core_copy(rd, o).wait_send()


def on_device(queries, views, positives, query_weight, owners, view_weight, view_kinds, kind_scale):
    rows, width = queries.shape
    vcols = views.shape[0]
    nchunk = rows // CHUNK
    sub = rows // 64
    half = width // 2
    nrow = rows // 128
    pos = positives.reshape(nrow, 128)
    qw = query_weight.reshape(nrow, 128)
    own = owners.reshape(NPB, 1, vcols)
    vw = view_weight.reshape(NPB, 1, vcols)
    kind = view_kinds.reshape(NPB, 1, vcols)
    vmem = pl.BlockSpec(memory_space=pltpu.VMEM)
    V = pltpu.VMEM
    dma = pltpu.SemaphoreType.DMA
    gq, gv, tg = pl.pallas_call(
        functools.partial(kernel, rows * NPB),
        out_shape=(
            jax.ShapeDtypeStruct((sub, width), F32),
            jax.ShapeDtypeStruct((vcols, width), F32),
            jax.ShapeDtypeStruct((8, 128), F32),
        ),
        in_specs=[pl.BlockSpec(memory_space=pltpu.SMEM), vmem, pl.BlockSpec(memory_space=pl.ANY)] + [vmem] * 5,
        out_specs=(vmem, vmem, vmem),
        scratch_shapes=[
            V((rows, width), BF16),
            V((width, 2 * rows), BF16),
            V((2, 4, 4, 2, sub, width), BF16),
            V((2 * vcols, width), BF16),
            V((2 * rows, 2 * vcols), F32),
            V((2 * rows, 2 * vcols), BF16),
            V((2, sub, width), F32),
            V((2, sub, width), BF16),
            V((2 * nrow, 128), F32),
            V((2 * nrow, 128), F32),
            V((2 * rows, 128), F32),
            V((2 * rows, 128), F32),
            V((2 * rows, 128), F32),
            V((4, NY, NX, sub, width), F32),
            V((4, NY, NX, sub, width), BF16),
            V((4, NY, NX, sub, width), BF16),
            V((4, NX, NY, sub, half), BF16),
            V((4, NY, NX, sub, half), BF16),
            V((4, NX, NY, sub, half), BF16),
            V((4, NY, NX, sub, half), BF16),
            V((4, NY, sub, half), BF16),
            V((4, NX, sub, half), BF16),
            V((4, NY, sub, half), BF16),
            V((4, NX, sub, half), BF16),
            V((4, NY, sub, half), F32),
            V((4, NX, sub, half), F32),
            V((4, sub, width), F32),
            V((3, sub, width), F32),
            V((2, width, vcols), F32),
            V((width, vcols), BF16),
            V((width, vcols), BF16),
            V((2, 2 * nchunk, vcols), F32),
            V((3, nrow, 128), F32),
            V((2, 2, 1, vcols), F32),
            V((2, 1, vcols), F32),
            V((NA, 2, nrow, 128), F32),
            V((NB, 2, nrow, 128), F32),
            V((2, nrow, 128), F32),
            V((NA, 8, 128), F32),
            V((NB, 8, 128), F32),
            V((2, 8, 128), F32),
            dma((nchunk,)), dma((2,)),
            dma((16,)), dma((16,)),
            dma((8,)), dma((8,)),
            dma((4,)), dma((4,)),
            dma((1,)), dma((1,)),
            dma((NA + NB,)), dma((NA + NB,)),
            dma((NA + NB + 1,)), dma((NA + NB + 1,)),
            dma((16,)), dma((16,)),
            dma((64,)), dma((64,)),
            dma((4,)), dma((4,)),
        ],
        compiler_params=pltpu.CompilerParams(collective_id=0, has_side_effects=True,
                                             vmem_limit_bytes=63 * 1024 * 1024),
    )(kind_scale, views, queries.reshape(4, 4, 4, sub, width), pos, qw, own, vw, kind)
    return gq, gv, tg[:3, 0]


def solution(mesh):
    in_specs = (P("pb", None), P(("vert", "pb"), None), P("pb"), P("pb"), P("vert"), P("vert"), P("vert"), P())
    out_specs = (P(("pb", "vert"), None), P(("vert", "pb"), None), P())
    return jax.shard_map(on_device, mesh=mesh, in_specs=in_specs, out_specs=out_specs, check_vma=False)
```

```python
import functools
import math

import jax
import jax.numpy as jnp
from jax import lax
from jax.experimental import pallas as pl
from jax.experimental.pallas import tpu as pltpu
from jax.sharding import PartitionSpec as P

MESH = pl.DeviceIdType.MESH
LOG2E = math.log2(math.e)
LN2 = math.log(2.0)
NPB = 4
NX = 4
NY = 4
NA = 8
NB = 8
CHUNK = 256
F32 = jnp.float32
BF16 = jnp.bfloat16


def kernel(total_queries, kscale_ref, views_hbm, q_hbm, pos_hbm, qw_hbm, own_hbm, vw_hbm, kind_hbm,
           gq_out, gv_out, tg_out,
           views_ref, pos_ref, qw_ref, own_ref, vw_ref, kind_ref, in_sem,
           qb, qt, qf, vb, S, H, qslice, qzs, pq, pqf, rep, qwrep, posrep, gown, csend, crecv,
           sa1, sb1, ra1, rb1, sa2, sb2, ra2, rb2, acca, accb, res, zres, gvt, zs, zr,
           colpart, rowpart, colx, colfin, rowa, rowb, rowc, rowfin, ta, tb, to, tp,
           qsem, slsem, ag_send, ag_recv, core_send, core_recv, vz_send, vz_recv,
           col_send, col_recv, row_send, row_recv, t_send, t_recv,
           c_send, c_recv, x_send, x_recv, z_send, z_recv):
    p = lax.axis_index("pb")
    v = lax.axis_index("vert")
    core = v % 2
    x = (v // 2) % NX
    y = (v // (2 * NX)) % NY
    zh = v // (2 * NX * NY)
    even = p % 2
    upper = p // 2
    mate = p + 1 - 2 * even
    far = (p + 2) % NPB
    a_me = v % NA
    b_me = upper * NY + y
    rows, width = qb.shape
    nchunk = rows // CHUNK
    vcols = views_ref.shape[0]
    half = width // 2
    sub = gown.shape[3]

    def vert_of(zh_, y_, x_, c_):
        return ((zh_ * NY + y_) * NX + x_) * 2 + c_

    def remote(src, dst, ssem, rsem, dev):
        return pltpu.make_async_remote_copy(src_ref=src, dst_ref=dst, send_sem=ssem, recv_sem=rsem,
                                            device_id=dev, device_id_type=MESH)

    here = (p, v)
    sends = []

    def go(copy):
        copy.start()
        sends.append(copy)

    sl_a = (y * NX + x) * 2 + core
    sl_b = 8 * NY + (x * NY + y) * 2 + core
    slices = []
    for i, sl in enumerate((sl_a, sl_b)):
        slices.append(pltpu.make_async_copy(q_hbm.at[sl // 16, (sl // 4) % 4, sl % 4], qslice.at[i], slsem.at[i]))
        slices[-1].start()

    small = [pltpu.make_async_copy(src, dst, in_sem.at[i]) for i, (src, dst) in enumerate((
        (views_hbm, views_ref), (pos_hbm, pos_ref), (qw_hbm, qw_ref), (own_hbm, own_ref), (vw_hbm, vw_ref),
        (kind_hbm, kind_ref)))]
    for copy in small:
        copy.start()

    def load(r):
        part = (r // 2, pl.ds((r % 2) * 2, 2))
        return pltpu.make_async_copy(q_hbm.at[part], gown.at[part], qsem.at[r])

    for r in range(nchunk):
        load(r).start()

    peers_a = [(p, (v // NA) * NA + (a_me + d) % NA) for d in range(1, NA)]
    peers_b = []
    for d in range(1, NB):
        i = (b_me + d) % NB
        peers_b.append(((i // NY) * 2 + even, vert_of(zh, i % NY, x, core)))
    over = (p, vert_of(1 - zh, y, x, core))
    peers = [over] + peers_a + peers_b + [(mate, v)]
    barrier = pltpu.get_barrier_semaphore()
    for dev in peers:
        pl.semaphore_signal(barrier, inc=1, device_id=dev, device_id_type=MESH)
    nrow = rows // 128
    for i in range(2):
        slices[i].wait()
        qzs[i] = qslice[i].astype(BF16)
    for copy in small:
        copy.wait()
    vb[0:vcols, :] = views_ref[...].astype(BF16)
    pq[0:nrow, :] = pos_ref[...].astype(F32)
    pq[nrow:2 * nrow, :] = qw_ref[...]
    pl.semaphore_wait(barrier, len(peers))

    def to_far(i, src, dst):
        return remote(src, dst, vz_send.at[i], vz_recv.at[i], (far, v))

    go(to_far(0, qzs.at[0], qf.at[0, y, x, core]))
    go(to_far(1, qzs.at[1], qf.at[1, x, y, core]))
    views_copy = remote(vb.at[pl.ds(0, vcols)], vb.at[pl.ds(vcols, vcols)], vz_send.at[2], vz_recv.at[2], (mate, v))
    go(views_copy)
    go(to_far(3, pq, pqf))

    def to_x(d):
        return (p, vert_of(zh, y, (x + d) % NX, core))

    def to_y(d):
        return (p, vert_of(zh, (y + d) % NY, x, core))

    twin = (p, vert_of(zh, y, x, 1 - core))

    k0, k1, k2 = kscale_ref[0], kscale_ref[1], kscale_ref[2]
    blocks = (p, mate)

    def scale_of(k):
        kind = kind_ref[k]
        return jnp.where(kind == 0, k0, jnp.where(kind == 1, k1, k2))

    scales = [scale_of(k) for k in blocks]
    scales2 = [s * LOG2E for s in scales]

    def cast_queries(r, carry):
        load(r).wait()
        block = gown[r // 2, pl.ds((r % 2) * 2, 2)].reshape(CHUNK, width)
        at = pl.multiple_of(r * CHUNK, CHUNK)
        qb[pl.ds(at, CHUNK), :] = block.astype(BF16)
        qt[:, pl.ds(at, CHUNK)] = block.T.astype(BF16)
        return carry

    lax.fori_loop(0, nchunk, cast_queries, 0)

    def score(q, at, ch, slots, row_at):
        tiles = []
        for sl in slots:
            cols = slice(sl * vcols, (sl + 1) * vcols)
            s = lax.dot_general(q, vb[cols, :], (((1,), (1,)), ((), ())),
                                preferred_element_type=F32) * scales2[sl]
            S[pl.ds(at, CHUNK), cols] = s
            peak = jnp.max(s, axis=0, keepdims=True)
            colpart[sl, pl.ds(ch, 1), :] = peak + jnp.log2(jnp.sum(jnp.exp2(s - peak), axis=0, keepdims=True))
            tiles += [s[:, h * 128:(h + 1) * 128] for h in range(vcols // 128)]
        m = functools.reduce(jnp.maximum, tiles)
        total = functools.reduce(jnp.add, [jnp.exp2(t - m) for t in tiles])
        for i in range(CHUNK // 128):
            mt = m[i * 128:(i + 1) * 128, :].T
            lt = total[i * 128:(i + 1) * 128, :].T
            peak = jnp.max(mt, axis=0, keepdims=True)
            lse = peak + jnp.log2(jnp.sum(lt * jnp.exp2(mt - peak), axis=0, keepdims=True))
            rowpart[row_at[0], pl.ds(row_at[1] * 2 + i, 1), :] = lse

    def own_pass(sl, first, last):
        def step(i, carry):
            for j in range(2):
                r = i * 2 + j
                at = pl.multiple_of(r * CHUNK, CHUNK)
                score(qb[pl.ds(at, CHUNK), :], at, r, (sl,), (sl, r))
            return carry

        lax.fori_loop(first // 2, last // 2, step, 0)

    def far_pass(parts):
        for h, o in parts:
            r = h * 4 + o
            q = qf[h, o].reshape(CHUNK, width)
            at = pl.multiple_of(rows + r * CHUNK, CHUNK)
            score(q, at, r + nchunk, (0, 1), (2, r))
            qt[:, pl.ds(at, CHUNK)] = q.T

    def got(ref, sem):
        remote(ref, ref, sem, sem, here).wait_recv()

    def spread(src, first, dst, at0):
        for r in range(nrow):
            dst[at0 + r * 128:at0 + (r + 1) * 128, :] = jnp.broadcast_to(src[first + r:first + r + 1, :], (128, 128)).T

    def slice_a(i, dest, ssem, rsem):
        go(remote(qf.at[0, y, i, core], qf.at[0, y, i, core], ag_send.at[ssem], ag_recv.at[rsem], dest))

    def slice_b(i, dest, ssem, rsem):
        go(remote(qf.at[1, x, i, core], qf.at[1, x, i, core], ag_send.at[ssem], ag_recv.at[rsem], dest))

    def second_a(k):
        i = (x + k) % NX
        for d in (1, 3, 2):
            slice_a(i, to_y(d), 8 + k * 4 + d, 8 + y * 4 + i)

    def second_b(k):
        i = (y + k) % NY
        for d in (1, 3, 2):
            slice_b(i, to_x(d), 24 + k * 4 + d, 24 + x * 4 + i)

    own_pass(0, 0, 2)
    got(qf.at[0, y, x, core], vz_recv.at[0])
    for d in (1, 3, 2):
        slice_a(x, to_x(d), d, x)
    second_a(0)
    got(qf.at[1, x, y, core], vz_recv.at[1])
    for d in (1, 3, 2):
        slice_b(y, to_y(d), 4 + d, 4 + y)
    second_b(0)
    own_pass(0, 2, 8)
    for k in (1, 3, 2):
        got(qf.at[0, y, (x + k) % NX, core], ag_recv.at[(x + k) % NX])
        second_a(k)
        got(qf.at[1, x, (y + k) % NY, core], ag_recv.at[4 + (y + k) % NY])
        second_b(k)

    def to_twin(h, o):
        part = qf.at[h, o, :, core]
        go(remote(part, part, core_send.at[h * 4 + o], core_recv.at[h * 4 + o], twin))

    def from_twin(h, o):
        got(qf.at[h, o, :, 1 - core], core_recv.at[h * 4 + o])

    def arrive(d):
        o = (y + d) % NY
        for k in (0, 1, 3, 2):
            i = (x + k) % NX
            got(qf.at[0, o, i, core], ag_recv.at[8 + o * 4 + i])
        to_twin(0, o)
        o = (x + d) % NX
        for k in (0, 1, 3, 2):
            i = (y + k) % NY
            got(qf.at[1, o, i, core], ag_recv.at[24 + o * 4 + i])
        to_twin(1, o)

    def far_step(d):
        from_twin(0, (y + d) % NY)
        from_twin(1, (x + d) % NX)
        far_pass([(0, (y + d) % NY), (1, (x + d) % NX)])

    to_twin(0, y)
    to_twin(1, x)
    spread(pq, 0, posrep, 0)
    spread(pq, nrow, qwrep, 0)
    got(vb.at[pl.ds(vcols, vcols)], vz_recv.at[2])
    own_pass(1, 0, 8)
    far_step(0)
    got(pqf, vz_recv.at[3])
    spread(pqf, 0, posrep, rows)
    spread(pqf, nrow, qwrep, rows)
    arrive(1)
    arrive(3)
    far_step(1)
    arrive(2)
    far_step(3)
    far_step(2)

    def log_sum(parts):
        m = functools.reduce(jnp.maximum, parts)
        return m + jnp.log2(functools.reduce(jnp.add, [jnp.exp2(t - m) for t in parts]))

    def exchange_a(buf, ssem, rsem, base):
        for d in range(1, NA):
            go(remote(buf.at[a_me], buf.at[a_me], ssem.at[base + d], rsem.at[base + a_me], peers_a[d - 1]))

    def exchange_b(buf, ssem, rsem, base):
        for d in range(1, NB):
            go(remote(buf.at[b_me], buf.at[b_me], ssem.at[base + d], rsem.at[base + b_me], peers_b[d - 1]))

    def collect(buf, rsem, base, me, n):
        for d in range(1, n):
            src = (me + d) % n
            got(buf.at[src], rsem.at[base + src])

    rowa[a_me, upper] = log_sum([rowpart[0], rowpart[1]])
    rowa[a_me, 1 - upper] = rowpart[2]
    exchange_a(rowa, row_send, row_recv, 0)
    for sl in range(2):
        part = colpart[sl]
        m = jnp.max(part, axis=0, keepdims=True)
        at = even if sl == 0 else 1 - even
        colx[even, at] = m + jnp.log2(jnp.sum(jnp.exp2(part - m), axis=0, keepdims=True))
    go(remote(colx.at[even], colx.at[even], col_send.at[0], col_recv.at[0], (mate, v)))
    collect(rowa, row_recv, 0, a_me, NA)
    rowb[b_me] = log_sum([rowa[i] for i in range(NA)])
    exchange_b(rowb, row_send, row_recv, NA)
    got(colx.at[1 - even], col_recv.at[0])
    for sl in range(2):
        at = even if sl == 0 else 1 - even
        colfin[sl] = log_sum([colx[0, at], colx[1, at]]) - jnp.log2(vw_ref[blocks[sl]])
    collect(rowb, row_recv, NA, b_me, NB)
    rowc[0] = log_sum([rowb[i] for i in range(NB)])
    go(remote(rowc.at[0], rowc.at[1], col_send.at[1], col_recv.at[1], over))
    got(rowc.at[1], col_recv.at[1])
    rowfin[...] = log_sum([rowc[0], rowc[1]])
    pqw = (pq, pqf)
    for b in range(2):
        at = upper if b == 0 else 1 - upper
        rowpart[b] = rowfin[at] - jnp.log2(pqw[b][nrow:2 * nrow, :])

    def spread_lse(b):
        for r in range(nrow):
            rep[b * rows + r * 128:b * rows + (r + 1) * 128, :] = jnp.broadcast_to(rowpart[b, r:r + 1, :], (128, 128)).T

    spread_lse(1)

    lane = lax.broadcasted_iota(jnp.int32, (CHUNK, 128), 1).astype(F32)
    row_id = lax.broadcasted_iota(jnp.int32, (CHUNK, 128), 0)
    ntile = 2 * vcols // 128
    per = vcols // 128

    def tile(arr, h):
        return arr[h // per][:, (h % per) * 128:(h % per + 1) * 128]

    weights = [vw_ref[k] for k in blocks]
    owners = [own_ref[k] for k in blocks]
    shifts = [colfin[0], colfin[1]]
    col0 = [(v * (NPB * vcols) + k * vcols).astype(F32) for k in blocks]
    rounds = [(1, 1 - zh), (1, zh), (0, 1 - zh), (0, zh)]

    def core_copy(rd, o):
        return remote(csend.at[rd, o], crecv.at[rd, o], c_send.at[rd * 4 + o], c_recv.at[rd * 4 + o], twin)

    def grad_step(rd, o, terms):
        b, z = rounds[rd]
        at = pl.multiple_of(b * rows + z * (rows // 2) + o * CHUNK, CHUNK)
        first_row = (p if b == 0 else far) * rows + z * (rows // 2) + o * CHUNK
        ra, rw, rp = rep[pl.ds(at, CHUNK), :], qwrep[pl.ds(at, CHUNK), :], posrep[pl.ds(at, CHUNK), :]
        out, pieces = [], []
        for h in range(ntile):
            s = S[pl.ds(at, CHUNK), h * 128:(h + 1) * 128]
            g = jnp.exp2(s - ra) + jnp.exp2(s - tile(shifts, h))
            col = lane + (col0[h // per] + (h % per) * 128)
            g = g - jnp.where(rp == col, rw, 0.0)
            g = g - jnp.where(row_id == tile(owners, h) - first_row, tile(weights, h), 0.0)
            pieces.append((g * tile(scales, h)).astype(BF16))
            out.append(terms[h] + jnp.sum(g * s, axis=0, keepdims=True))
        hh = jnp.concatenate(pieces, axis=1)
        H[pl.ds(at, CHUNK), :] = hh
        acc = jnp.dot(hh, vb[...], preferred_element_type=F32).reshape(NX, 2, sub, width)
        first, second = acc[:, 0], acc[:, 1]
        gown[rd, o] = jnp.where(core == 0, first, second)
        csend[rd, o] = jnp.where(core == 0, second, first).astype(BF16)
        core_copy(rd, o).start()
        return tuple(out)

    def grad_half(rd, part, terms):
        for j in range(2):
            terms = grad_step(rd, part * 2 + j, terms)
        return terms

    def fold_core(rd):
        def step(o, carry):
            core_copy(rd, o).wait_recv()
            for i in range(NX):
                val = gown[rd, o, i] + crecv[rd, o, i].astype(F32)
                gown[rd, o, i] = val
                sa1[rd, i, o] = val[:, :half].astype(BF16)
                sb1[rd, o, i] = val[:, half:].astype(BF16)
            return carry

        lax.fori_loop(0, NY, step, 0)
        for d in (1, 3, 2):
            go(remote(sa1.at[rd, (x + d) % NX], ra1.at[rd, x], x_send.at[rd * 16 + d], x_recv.at[rd * 16 + x], to_x(d)))
            go(remote(sb1.at[rd, (y + d) % NY], rb1.at[rd, y], x_send.at[rd * 16 + 4 + d], x_recv.at[rd * 16 + 4 + y],
                      to_y(d)))

    def fold_first(rd):
        for d in (1, 3, 2):
            got(ra1.at[rd, (x + d) % NX], x_recv.at[rd * 16 + (x + d) % NX])
        for o in range(NY):
            val = gown[rd, o, x][:, :half]
            for d in range(1, NX):
                val = val + ra1[rd, (x + d) % NX, o].astype(F32)
            acca[rd, o] = val
            sa2[rd, o] = val.astype(BF16)
        for d in (1, 3, 2):
            go(remote(sa2.at[rd, (y + d) % NY], ra2.at[rd, y], x_send.at[rd * 16 + 8 + d], x_recv.at[rd * 16 + 8 + y],
                      to_y(d)))
        for d in (1, 3, 2):
            got(rb1.at[rd, (y + d) % NY], x_recv.at[rd * 16 + 4 + (y + d) % NY])
        for i in range(NX):
            val = gown[rd, y, i][:, half:]
            for d in range(1, NY):
                val = val + rb1[rd, (y + d) % NY, i].astype(F32)
            accb[rd, i] = val
            sb2[rd, i] = val.astype(BF16)
        for d in (1, 3, 2):
            go(remote(sb2.at[rd, (x + d) % NX], rb2.at[rd, x], x_send.at[rd * 16 + 12 + d],
                      x_recv.at[rd * 16 + 12 + x], to_x(d)))

    def fold_second(rd):
        for d in (1, 3, 2):
            got(ra2.at[rd, (y + d) % NY], x_recv.at[rd * 16 + 8 + (y + d) % NY])
        val = acca[rd, y]
        for d in range(1, NY):
            val = val + ra2[rd, (y + d) % NY].astype(F32)
        res[rd, :, :half] = val
        for d in (1, 3, 2):
            got(rb2.at[rd, (x + d) % NX], x_recv.at[rd * 16 + 12 + (x + d) % NX])
        val = accb[rd, x]
        for d in range(1, NX):
            val = val + rb2[rd, (x + d) % NX].astype(F32)
        res[rd, :, half:] = val
        if rd < 2:
            go(remote(res.at[rd], zres.at[rd], z_send.at[rd], z_recv.at[rd], (far, v)))
        if rd == 2:
            got(zres.at[0], z_recv.at[0])
            res[2] = res[2] + zres[0]
            go(remote(res.at[2], zres.at[2], z_send.at[2], z_recv.at[2], over))

    def grad_views(sl):
        def step(i, carry):
            at = pl.multiple_of(i * CHUNK, CHUNK)
            gvt[sl, pl.ds(at, CHUNK), :] = jnp.dot(qt[pl.ds(at, CHUNK), :], H[:, sl * vcols:(sl + 1) * vcols],
                                                   preferred_element_type=F32)
            return carry

        lax.fori_loop(0, width // CHUNK, step, 0)

    terms = (jnp.zeros((1, 128), F32),) * ntile
    terms = grad_half(0, 0, terms)
    terms = grad_half(0, 1, terms)
    spread_lse(0)
    fold_core(0)
    terms = grad_half(1, 0, terms)
    terms = grad_half(1, 1, terms)
    terms = grad_half(2, 0, terms)
    fold_core(1)
    terms = grad_half(2, 1, terms)
    fold_first(0)
    terms = grad_half(3, 0, terms)
    fold_core(2)
    terms = grad_half(3, 1, terms)
    grad_views(1)
    zs[...] = gvt[1].astype(BF16)
    go(remote(zs, zr, z_send.at[3], z_recv.at[3], (mate, v)))
    fold_core(3)

    kinds = []
    for t in range(3):
        kinds.append(functools.reduce(jnp.add, [
            jnp.where(tile([kind_ref[k] for k in blocks], h) == t, terms[h], 0.0) for h in range(ntile)]))
    ta[a_me] = jnp.concatenate(kinds + [jnp.zeros((5, 128), F32)], axis=0) * (LN2 / total_queries)
    exchange_a(ta, t_send, t_recv, 0)

    fold_first(1)
    grad_views(0)
    fold_second(0)
    collect(ta, t_recv, 0, a_me, NA)
    tb[b_me] = functools.reduce(jnp.add, [ta[i] for i in range(NA)])
    exchange_b(tb, t_send, t_recv, NA)
    fold_first(2)
    fold_second(1)
    collect(tb, t_recv, NA, b_me, NB)
    to[0] = functools.reduce(jnp.add, [tb[i] for i in range(NB)])
    go(remote(to.at[0], to.at[1], t_send.at[NA + NB], t_recv.at[NA + NB], over))
    fold_second(2)
    fold_first(3)
    got(zr, z_recv.at[3])
    gv_out[...] = (gvt[0] + zr[...].astype(F32)).T
    got(to.at[1], t_recv.at[NA + NB])
    tp[0] = to[0] + to[1]
    go(remote(tp.at[0], tp.at[1], t_send.at[NA + NB + 1], t_recv.at[NA + NB + 1], (mate, v)))
    fold_second(3)
    got(tp.at[1], t_recv.at[NA + NB + 1])
    sums = jnp.sum(tp[0] + tp[1], axis=1, keepdims=True)
    tg_out[...] = jnp.broadcast_to(sums, tg_out.shape)
    got(zres.at[1], z_recv.at[1])
    total = res[3] + zres[1]
    got(zres.at[2], z_recv.at[2])
    gq_out[...] = total + zres[2]

    for copy in sends:
        copy.wait_send()
    for rd in range(4):
        for o in range(4):
            core_copy(rd, o).wait_send()


def hand_over(gq_in, gv_in, tg_in, gq_out, gv_out, tg_out):
    gq_out[...] = gq_in[...]
    gv_out[...] = gv_in[...]
    for i in range(3):
        tg_out[i] = tg_in[i, 0]


def on_device(queries, views, positives, query_weight, owners, view_weight, view_kinds, kind_scale):
    rows, width = queries.shape
    vcols = views.shape[0]
    nchunk = rows // CHUNK
    sub = rows // 64
    half = width // 2
    nrow = rows // 128
    pos = positives.reshape(nrow, 128)
    qw = query_weight.reshape(nrow, 128)
    own = owners.reshape(NPB, 1, vcols)
    vw = view_weight.reshape(NPB, 1, vcols)
    kind = view_kinds.reshape(NPB, 1, vcols)
    vmem = pl.BlockSpec(memory_space=pltpu.VMEM)
    V = pltpu.VMEM
    dma = pltpu.SemaphoreType.DMA
    gq, gv, tg = pl.pallas_call(
        functools.partial(kernel, rows * NPB),
        out_shape=(
            jax.ShapeDtypeStruct((sub, width), F32),
            jax.ShapeDtypeStruct((vcols, width), F32),
            jax.ShapeDtypeStruct((8, 128), F32),
        ),
        in_specs=[pl.BlockSpec(memory_space=pltpu.SMEM)] + [pl.BlockSpec(memory_space=pl.ANY)] * 7,
        out_specs=(vmem, vmem, vmem),
        scratch_shapes=[
            V((vcols, width), F32),
            V((nrow, 128), jnp.int32),
            V((nrow, 128), F32),
            V((NPB, 1, vcols), jnp.int32),
            V((NPB, 1, vcols), F32),
            V((NPB, 1, vcols), jnp.int32),
            dma((6,)),
            V((rows, width), BF16),
            V((width, 2 * rows), BF16),
            V((2, 4, 4, 2, sub, width), BF16),
            V((2 * vcols, width), BF16),
            V((2 * rows, 2 * vcols), F32),
            V((2 * rows, 2 * vcols), BF16),
            V((2, sub, width), F32),
            V((2, sub, width), BF16),
            V((2 * nrow, 128), F32),
            V((2 * nrow, 128), F32),
            V((2 * rows, 128), F32),
            V((2 * rows, 128), F32),
            V((2 * rows, 128), F32),
            V((4, NY, NX, sub, width), F32),
            V((4, NY, NX, sub, width), BF16),
            V((4, NY, NX, sub, width), BF16),
            V((4, NX, NY, sub, half), BF16),
            V((4, NY, NX, sub, half), BF16),
            V((4, NX, NY, sub, half), BF16),
            V((4, NY, NX, sub, half), BF16),
            V((4, NY, sub, half), BF16),
            V((4, NX, sub, half), BF16),
            V((4, NY, sub, half), BF16),
            V((4, NX, sub, half), BF16),
            V((4, NY, sub, half), F32),
            V((4, NX, sub, half), F32),
            V((4, sub, width), F32),
            V((3, sub, width), F32),
            V((2, width, vcols), F32),
            V((width, vcols), BF16),
            V((width, vcols), BF16),
            V((2, 2 * nchunk, vcols), F32),
            V((3, nrow, 128), F32),
            V((2, 2, 1, vcols), F32),
            V((2, 1, vcols), F32),
            V((NA, 2, nrow, 128), F32),
            V((NB, 2, nrow, 128), F32),
            V((2, 2, nrow, 128), F32),
            V((2, nrow, 128), F32),
            V((NA, 8, 128), F32),
            V((NB, 8, 128), F32),
            V((2, 8, 128), F32),
            V((2, 8, 128), F32),
            dma((nchunk,)), dma((2,)),
            dma((40,)), dma((40,)),
            dma((8,)), dma((8,)),
            dma((4,)), dma((4,)),
            dma((2,)), dma((2,)),
            dma((NA + NB,)), dma((NA + NB,)),
            dma((NA + NB + 2,)), dma((NA + NB + 2,)),
            dma((16,)), dma((16,)),
            dma((64,)), dma((64,)),
            dma((4,)), dma((4,)),
        ],
        compiler_params=pltpu.CompilerParams(collective_id=0, has_side_effects=True,
                                             vmem_limit_bytes=63 * 1024 * 1024),
    )(kind_scale, views, queries.reshape(4, 4, 4, sub, width), pos, qw, own, vw, kind)
    smem = pl.BlockSpec(memory_space=pltpu.SMEM)
    return pl.pallas_call(
        hand_over,
        out_shape=(
            jax.ShapeDtypeStruct(gq.shape, F32),
            jax.ShapeDtypeStruct(gv.shape, F32),
            jax.ShapeDtypeStruct(kind_scale.shape, F32),
        ),
        in_specs=[vmem, vmem, smem],
        out_specs=(vmem, vmem, smem),
    )(gq, gv, tg)


def solution(mesh):
    in_specs = (P("pb", None), P(("vert", "pb"), None), P("pb"), P("pb"), P("vert"), P("vert"), P("vert"), P())
    out_specs = (P(("pb", "vert"), None), P(("vert", "pb"), None), P())
    return jax.shard_map(on_device, mesh=mesh, in_specs=in_specs, out_specs=out_specs, check_vma=False)
```

```python
import functools
import math

import jax
import jax.numpy as jnp
from jax import lax
from jax.experimental import pallas as pl
from jax.experimental.pallas import tpu as pltpu
from jax.sharding import PartitionSpec as P

MESH = pl.DeviceIdType.MESH
LOG2E = math.log2(math.e)
LN2 = math.log(2.0)
NPB = 4
NX = 4
NY = 4
NA = 8
NB = 8
CHUNK = 256
F32 = jnp.float32
BF16 = jnp.bfloat16


def kernel(total_queries, kscale_ref, views_hbm, q_hbm, pos_hbm, qw_hbm, own_hbm, vw_hbm, kind_hbm,
           gq_out, gv_out, tg_out,
           pos_ref, qw_ref, own_ref, vw_ref, kind_ref, in_sem,
           qb, qt, qf, vb, S, H, qslice, qzs, pq, pqf, rep, qwrep, posrep, gown, csend, crecv,
           sa1, sb1, ra1, rb1, sa2, sb2, ra2, rb2, res, zout, zres, gvt, zs, zr,
           colpart, rowpart, colx, colfin, rowa, rowb, rowc, rowfin, ta, tb, to, tp,
           qsem, slsem, ag_send, ag_recv, core_send, core_recv, vz_send, vz_recv,
           col_send, col_recv, row_send, row_recv, t_send, t_recv,
           c_send, c_recv, x_send, x_recv, z_send, z_recv):
    p = lax.axis_index("pb")
    v = lax.axis_index("vert")
    core = v % 2
    x = (v // 2) % NX
    y = (v // (2 * NX)) % NY
    zh = v // (2 * NX * NY)
    even = p % 2
    upper = p // 2
    mate = p + 1 - 2 * even
    far = (p + 2) % NPB
    a_me = zh * NX + x
    b_me = upper * NY + y
    rows, width = qb.shape
    nchunk = rows // CHUNK
    vcols = own_ref.shape[2]
    half = width // 2
    sub = gown.shape[3]

    def vert_of(zh_, y_, x_, c_):
        return ((zh_ * NY + y_) * NX + x_) * 2 + c_

    def remote(src, dst, ssem, rsem, dev):
        return pltpu.make_async_remote_copy(src_ref=src, dst_ref=dst, send_sem=ssem, recv_sem=rsem,
                                            device_id=dev, device_id_type=MESH)

    here = (p, v)
    sends = []

    def go(copy):
        copy.start()
        sends.append(copy)

    sl_a = (y * NX + x) * 2 + core
    sl_b = 8 * NY + (x * NY + y) * 2 + core
    slices = []
    for i, sl in enumerate((sl_a, sl_b)):
        slices.append(pltpu.make_async_copy(q_hbm.at[sl // 16, (sl // 4) % 4, sl % 4], qslice.at[i], slsem.at[i]))
        slices[-1].start()

    small = [pltpu.make_async_copy(src, dst, in_sem.at[i]) for i, (src, dst) in enumerate((
        (views_hbm, csend.at[0, pl.ds(0, 2)]), (pos_hbm, pos_ref), (qw_hbm, qw_ref), (own_hbm, own_ref), (vw_hbm, vw_ref),
        (kind_hbm, kind_ref)))]
    for copy in small:
        copy.start()

    def load(r):
        part = (r // 2, pl.ds((r % 2) * 2, 2))
        return pltpu.make_async_copy(q_hbm.at[part], gown.at[part], qsem.at[r])

    for r in range(nchunk):
        load(r).start()

    peers_a = []
    for d in range(1, NA):
        i = (a_me + d) % NA
        peers_a.append((p, vert_of(i // NX, y, i % NX, core)))
    peers_b = []
    for d in range(1, NB):
        i = (b_me + d) % NB
        peers_b.append(((i // NY) * 2 + even, vert_of(zh, i % NY, x, core)))
    over = (p, vert_of(1 - zh, y, x, core))
    far_over = (far, vert_of(1 - zh, y, x, core))
    twin = (p, vert_of(zh, y, x, 1 - core))
    peers = peers_a + peers_b + [twin, (mate, v), far_over]
    barrier = pltpu.get_barrier_semaphore()
    for dev in peers:
        pl.semaphore_signal(barrier, inc=1, device_id=dev, device_id_type=MESH)
    nrow = rows // 128
    for i in range(2):
        slices[i].wait()
        qzs[i] = qslice[i].astype(BF16)
    for copy in small:
        copy.wait()
    vb[0:vcols, :] = csend[0, 0:2].reshape(vcols, width).astype(BF16)
    pq[0:nrow, :] = pos_ref[...].astype(F32)
    pq[nrow:2 * nrow, :] = qw_ref[...]
    pl.semaphore_wait(barrier, len(peers))

    def to_far(i, src, dst):
        return remote(src, dst, vz_send.at[i], vz_recv.at[i], (far, v))

    go(to_far(0, qzs.at[0], qf.at[0, y, x, core]))
    go(to_far(1, qzs.at[1], qf.at[1, x, y, core]))
    views_copy = remote(vb.at[pl.ds(0, vcols)], vb.at[pl.ds(vcols, vcols)], vz_send.at[2], vz_recv.at[2], (mate, v))
    go(views_copy)
    go(to_far(3, pq, pqf))

    def to_x(d):
        return (p, vert_of(zh, y, (x + d) % NX, core))

    def to_y(d):
        return (p, vert_of(zh, (y + d) % NY, x, core))

    k0, k1, k2 = kscale_ref[0], kscale_ref[1], kscale_ref[2]
    blocks = (p, mate)

    def scale_of(k):
        kind = kind_ref[k]
        return jnp.where(kind == 0, k0, jnp.where(kind == 1, k1, k2))

    scales = [scale_of(k) for k in blocks]
    scales2 = [s * LOG2E for s in scales]

    def cast_queries(r, carry):
        load(r).wait()
        block = gown[r // 2, pl.ds((r % 2) * 2, 2)].reshape(CHUNK, width)
        at = pl.multiple_of(r * CHUNK, CHUNK)
        qb[pl.ds(at, CHUNK), :] = block.astype(BF16)
        return carry

    lax.fori_loop(0, nchunk, cast_queries, 0)

    def score(q, at, ch, slots, row_at):
        tiles = []
        for sl in slots:
            cols = slice(sl * vcols, (sl + 1) * vcols)
            s = lax.dot_general(q, vb[cols, :], (((1,), (1,)), ((), ())),
                                preferred_element_type=F32) * scales2[sl]
            S[pl.ds(at, CHUNK), cols] = s
            peak = jnp.max(s, axis=0, keepdims=True)
            colpart[sl, pl.ds(ch, 1), :] = peak + jnp.log2(jnp.sum(jnp.exp2(s - peak), axis=0, keepdims=True))
            tiles += [s[:, h * 128:(h + 1) * 128] for h in range(vcols // 128)]
        m = functools.reduce(jnp.maximum, tiles)
        total = functools.reduce(jnp.add, [jnp.exp2(t - m) for t in tiles])
        for i in range(CHUNK // 128):
            mt = m[i * 128:(i + 1) * 128, :].T
            lt = total[i * 128:(i + 1) * 128, :].T
            peak = jnp.max(mt, axis=0, keepdims=True)
            lse = peak + jnp.log2(jnp.sum(lt * jnp.exp2(mt - peak), axis=0, keepdims=True))
            rowpart[row_at[0], pl.ds(row_at[1] * 2 + i, 1), :] = lse

    def own_pass(sl, first, last):
        def step(i, carry):
            for j in range(2):
                r = i * 2 + j
                at = pl.multiple_of(r * CHUNK, CHUNK)
                score(qb[pl.ds(at, CHUNK), :], at, r, (sl,), (sl, r))
            return carry

        lax.fori_loop(first // 2, last // 2, step, 0)

    def far_pass(parts):
        for h, o in parts:
            r = h * 4 + o
            q = qf[h, o].reshape(CHUNK, width)
            at = pl.multiple_of(rows + r * CHUNK, CHUNK)
            score(q, at, r + nchunk, (0, 1), (2, r))

    def got(ref, sem):
        remote(ref, ref, sem, sem, here).wait_recv()

    def spread(src, first, dst, at0):
        for r in range(nrow):
            dst[at0 + r * 128:at0 + (r + 1) * 128, :] = jnp.broadcast_to(src[first + r:first + r + 1, :], (128, 128)).T

    def slice_a(i, dest, ssem, rsem):
        go(remote(qf.at[0, y, i, core], qf.at[0, y, i, core], ag_send.at[ssem], ag_recv.at[rsem], dest))

    def slice_b(i, dest, ssem, rsem):
        go(remote(qf.at[1, x, i, core], qf.at[1, x, i, core], ag_send.at[ssem], ag_recv.at[rsem], dest))

    def second_a(k):
        i = (x + k) % NX
        for d in (1, 3, 2):
            slice_a(i, to_y(d), 8 + k * 4 + d, 8 + y * 4 + i)

    def second_b(k):
        i = (y + k) % NY
        for d in (1, 3, 2):
            slice_b(i, to_x(d), 24 + k * 4 + d, 24 + x * 4 + i)

    own_pass(0, 0, 2)
    got(qf.at[0, y, x, core], vz_recv.at[0])
    for d in (1, 3, 2):
        slice_a(x, to_x(d), d, x)
    second_a(0)
    got(qf.at[1, x, y, core], vz_recv.at[1])
    for d in (1, 3, 2):
        slice_b(y, to_y(d), 4 + d, 4 + y)
    second_b(0)
    own_pass(0, 2, 8)
    for k in (1, 3, 2):
        got(qf.at[0, y, (x + k) % NX, core], ag_recv.at[(x + k) % NX])
        second_a(k)
        got(qf.at[1, x, (y + k) % NY, core], ag_recv.at[4 + (y + k) % NY])
        second_b(k)

    def to_twin(h, o):
        part = qf.at[h, o, :, core]
        go(remote(part, part, core_send.at[h * 4 + o], core_recv.at[h * 4 + o], twin))

    def from_twin(h, o):
        got(qf.at[h, o, :, 1 - core], core_recv.at[h * 4 + o])

    def arrive(d):
        o = (y + d) % NY
        for k in (0, 1, 3, 2):
            i = (x + k) % NX
            got(qf.at[0, o, i, core], ag_recv.at[8 + o * 4 + i])
        to_twin(0, o)
        o = (x + d) % NX
        for k in (0, 1, 3, 2):
            i = (y + k) % NY
            got(qf.at[1, o, i, core], ag_recv.at[24 + o * 4 + i])
        to_twin(1, o)

    def far_step(d):
        from_twin(0, (y + d) % NY)
        from_twin(1, (x + d) % NX)
        far_pass([(0, (y + d) % NY), (1, (x + d) % NX)])

    to_twin(0, y)
    to_twin(1, x)
    got(vb.at[pl.ds(vcols, vcols)], vz_recv.at[2])
    own_pass(1, 0, 8)
    far_step(0)
    got(pqf, vz_recv.at[3])
    arrive(1)
    arrive(3)
    far_step(1)
    arrive(2)
    far_step(3)
    far_step(2)

    def log_sum(parts):
        m = functools.reduce(jnp.maximum, parts)
        return m + jnp.log2(functools.reduce(jnp.add, [jnp.exp2(t - m) for t in parts]))

    def exchange_a(buf, ssem, rsem, base):
        for d in range(1, NA):
            go(remote(buf.at[a_me], buf.at[a_me], ssem.at[base + d], rsem.at[base + a_me], peers_a[d - 1]))

    def exchange_b(buf, ssem, rsem, base):
        for d in range(1, NB):
            go(remote(buf.at[b_me], buf.at[b_me], ssem.at[base + d], rsem.at[base + b_me], peers_b[d - 1]))

    def collect(buf, rsem, base, me, n):
        for d in range(1, n):
            src = (me + d) % n
            got(buf.at[src], rsem.at[base + src])

    rowc[0, upper] = log_sum([rowpart[0], rowpart[1]])
    rowc[0, 1 - upper] = rowpart[2]
    go(remote(rowc.at[0], rowc.at[1], col_send.at[1], col_recv.at[1], twin))
    for sl in range(2):
        part = colpart[sl]
        m = jnp.max(part, axis=0, keepdims=True)
        at = even if sl == 0 else 1 - even
        colx[even, at] = m + jnp.log2(jnp.sum(jnp.exp2(part - m), axis=0, keepdims=True))
    go(remote(colx.at[even], colx.at[even], col_send.at[0], col_recv.at[0], (mate, v)))
    got(rowc.at[1], col_recv.at[1])
    rowa[a_me] = log_sum([rowc[0], rowc[1]])
    exchange_a(rowa, row_send, row_recv, 0)

    def turn_own(i, carry):
        for j in range(2):
            at = pl.multiple_of((i * 2 + j) * CHUNK, CHUNK)
            qt[:, pl.ds(at, CHUNK)] = qb[pl.ds(at, CHUNK), :].T
        return carry

    def turn_far(i, carry):
        for j in range(2):
            r = i * 2 + j
            at = pl.multiple_of(rows + r * CHUNK, CHUNK)
            qt[:, pl.ds(at, CHUNK)] = qf[r // 4, r % 4].reshape(CHUNK, width).T
        return carry

    lax.fori_loop(0, nchunk // 2, turn_own, 0)
    spread(pqf, 0, posrep, rows)
    spread(pqf, nrow, qwrep, rows)
    collect(rowa, row_recv, 0, a_me, NA)
    rowb[b_me] = log_sum([rowa[i] for i in range(NA)])
    exchange_b(rowb, row_send, row_recv, NA)
    got(colx.at[1 - even], col_recv.at[0])
    for sl in range(2):
        at = even if sl == 0 else 1 - even
        colfin[sl] = log_sum([colx[0, at], colx[1, at]]) - jnp.log2(vw_ref[blocks[sl]])
    lax.fori_loop(0, nchunk // 2, turn_far, 0)
    spread(pq, 0, posrep, 0)
    spread(pq, nrow, qwrep, 0)
    collect(rowb, row_recv, NA, b_me, NB)
    rowfin[...] = log_sum([rowb[i] for i in range(NB)])
    pqw = (pq, pqf)
    for b in range(2):
        at = upper if b == 0 else 1 - upper
        rowpart[b] = rowfin[at] - jnp.log2(pqw[b][nrow:2 * nrow, :])

    def spread_lse(b):
        for r in range(nrow):
            rep[b * rows + r * 128:b * rows + (r + 1) * 128, :] = jnp.broadcast_to(rowpart[b, r:r + 1, :], (128, 128)).T

    spread_lse(1)

    lane = lax.broadcasted_iota(jnp.int32, (CHUNK, 128), 1).astype(F32)
    row_id = lax.broadcasted_iota(jnp.int32, (CHUNK, 128), 0)
    ntile = 2 * vcols // 128
    per = vcols // 128

    def tile(arr, h):
        return arr[h // per][:, (h % per) * 128:(h % per + 1) * 128]

    weights = [vw_ref[k] for k in blocks]
    owners = [own_ref[k] for k in blocks]
    shifts = [colfin[0], colfin[1]]
    col0 = [(v * (NPB * vcols) + k * vcols).astype(F32) for k in blocks]
    rounds = [(1, 1 - zh), (0, 1 - zh), (1, zh), (0, zh)]

    def core_copy(rd, o):
        return remote(csend.at[rd, o], crecv.at[rd, o], c_send.at[rd * 4 + o], c_recv.at[rd * 4 + o], twin)

    def grad_step(rd, o, terms):
        b, z = rounds[rd]
        at = pl.multiple_of(b * rows + z * (rows // 2) + o * CHUNK, CHUNK)
        first_row = (p if b == 0 else far) * rows + z * (rows // 2) + o * CHUNK
        ra, rw, rp = rep[pl.ds(at, CHUNK), :], qwrep[pl.ds(at, CHUNK), :], posrep[pl.ds(at, CHUNK), :]
        out, pieces = [], []
        for h in range(ntile):
            s = S[pl.ds(at, CHUNK), h * 128:(h + 1) * 128]
            g = jnp.exp2(s - ra) + jnp.exp2(s - tile(shifts, h))
            col = lane + (col0[h // per] + (h % per) * 128)
            g = g - jnp.where(rp == col, rw, 0.0)
            g = g - jnp.where(row_id == tile(owners, h) - first_row, tile(weights, h), 0.0)
            pieces.append((g * tile(scales, h)).astype(BF16))
            out.append(terms[h] + jnp.sum(g * s, axis=0, keepdims=True))
        hh = jnp.concatenate(pieces, axis=1)
        H[pl.ds(at, CHUNK), :] = hh
        acc = jnp.dot(hh, vb[...], preferred_element_type=F32).reshape(NX, 2, sub, width)
        first, second = acc[:, 0], acc[:, 1]
        gown[rd, o] = jnp.where(core == 0, first, second)
        csend[rd, o] = jnp.where(core == 0, second, first)
        core_copy(rd, o).start()
        return tuple(out)

    def grad_half(rd, part, terms):
        for j in range(2):
            terms = grad_step(rd, part * 2 + j, terms)
        return terms

    def fold_core(rd):
        def step(o, carry):
            core_copy(rd, o).wait_recv()
            for i in range(NX):
                val = gown[rd, o, i] + crecv[rd, o, i]
                gown[rd, o, i] = val
                sa1[rd, i, o] = val[:, :half].astype(BF16)
                sb1[rd, o, i] = val[:, half:].astype(BF16)
            return carry

        lax.fori_loop(0, NY, step, 0)
        for d in (1, 3, 2):
            go(remote(sa1.at[rd, (x + d) % NX], ra1.at[rd, x], x_send.at[rd * 16 + d], x_recv.at[rd * 16 + x], to_x(d)))
            go(remote(sb1.at[rd, (y + d) % NY], rb1.at[rd, y], x_send.at[rd * 16 + 4 + d], x_recv.at[rd * 16 + 4 + y],
                      to_y(d)))

    def fold_first(rd):
        for d in (1, 3, 2):
            got(ra1.at[rd, (x + d) % NX], x_recv.at[rd * 16 + (x + d) % NX])
        for o in range(NY):
            val = gown[rd, o, x][:, :half]
            for d in range(1, NX):
                val = val + ra1[rd, (x + d) % NX, o].astype(F32)
            gown[rd, o, x, :, 0:half] = val
            sa2[rd, o] = val.astype(BF16)
        for d in (1, 3, 2):
            go(remote(sa2.at[rd, (y + d) % NY], ra2.at[rd, y], x_send.at[rd * 16 + 8 + d], x_recv.at[rd * 16 + 8 + y],
                      to_y(d)))
        for d in (1, 3, 2):
            got(rb1.at[rd, (y + d) % NY], x_recv.at[rd * 16 + 4 + (y + d) % NY])
        for i in range(NX):
            val = gown[rd, y, i][:, half:]
            for d in range(1, NY):
                val = val + rb1[rd, (y + d) % NY, i].astype(F32)
            gown[rd, y, i, :, half:width] = val
            sb2[rd, i] = val.astype(BF16)
        for d in (1, 3, 2):
            go(remote(sb2.at[rd, (x + d) % NX], rb2.at[rd, x], x_send.at[rd * 16 + 12 + d],
                      x_recv.at[rd * 16 + 12 + x], to_x(d)))

    def fold_second(rd):
        for d in (1, 3, 2):
            got(ra2.at[rd, (y + d) % NY], x_recv.at[rd * 16 + 8 + (y + d) % NY])
        val = gown[rd, y, x, :, 0:half]
        for d in range(1, NY):
            val = val + ra2[rd, (y + d) % NY].astype(F32)
        res[rd, :, :half] = val
        for d in (1, 3, 2):
            got(rb2.at[rd, (x + d) % NX], x_recv.at[rd * 16 + 12 + (x + d) % NX])
        val = gown[rd, y, x, :, half:width]
        for d in range(1, NX):
            val = val + rb2[rd, (x + d) % NX].astype(F32)
        res[rd, :, half:] = val
        if rd < 3:
            zout[rd] = res[rd].astype(BF16)
            go(remote(zout.at[rd], zres.at[rd], z_send.at[rd], z_recv.at[rd], (far_over, over, (far, v))[rd]))

    def grad_views(sl):
        def step(i, carry):
            at = pl.multiple_of(i * CHUNK, CHUNK)
            gvt[sl, pl.ds(at, CHUNK), :] = jnp.dot(qt[pl.ds(at, CHUNK), :], H[:, sl * vcols:(sl + 1) * vcols],
                                                   preferred_element_type=F32)
            return carry

        lax.fori_loop(0, width // CHUNK, step, 0)

    terms = (jnp.zeros((1, 128), F32),) * ntile
    terms = grad_half(0, 0, terms)
    terms = grad_half(0, 1, terms)
    spread_lse(0)
    fold_core(0)
    terms = grad_half(1, 0, terms)
    terms = grad_half(1, 1, terms)
    terms = grad_half(2, 0, terms)
    fold_core(1)
    terms = grad_half(2, 1, terms)
    terms = grad_half(3, 0, terms)
    fold_core(2)
    terms = grad_half(3, 1, terms)

    kinds = []
    for t in range(3):
        kinds.append(functools.reduce(jnp.add, [
            jnp.where(tile([kind_ref[k] for k in blocks], h) == t, terms[h], 0.0) for h in range(ntile)]))
    to[0] = jnp.concatenate(kinds + [jnp.zeros((5, 128), F32)], axis=0) * (LN2 / total_queries)
    go(remote(to.at[0], to.at[1], t_send.at[NA + NB], t_recv.at[NA + NB], twin))
    fold_first(0)
    got(to.at[1], t_recv.at[NA + NB])
    ta[a_me] = to[0] + to[1]
    exchange_a(ta, t_send, t_recv, 0)
    fold_core(3)
    grad_views(1)
    zs[...] = gvt[1].astype(BF16)
    go(remote(zs, zr, z_send.at[3], z_recv.at[3], (mate, v)))
    fold_first(1)
    collect(ta, t_recv, 0, a_me, NA)
    tb[b_me] = functools.reduce(jnp.add, [ta[i] for i in range(NA)])
    exchange_b(tb, t_send, t_recv, NA)
    fold_second(0)
    grad_views(0)
    fold_first(2)
    fold_second(1)
    collect(tb, t_recv, NA, b_me, NB)
    tp[0] = functools.reduce(jnp.add, [tb[i] for i in range(NB)])
    go(remote(tp.at[0], tp.at[1], t_send.at[NA + NB + 1], t_recv.at[NA + NB + 1], (mate, v)))
    fold_first(3)
    fold_second(2)
    got(zr, z_recv.at[3])
    gv_out[...] = (gvt[0] + zr[...].astype(F32)).T
    got(tp.at[1], t_recv.at[NA + NB + 1])
    sums = jnp.sum(tp[0] + tp[1], axis=1, keepdims=True)
    tg_out[...] = jnp.broadcast_to(sums, tg_out.shape)
    fold_second(3)
    total = res[3]
    for i in range(3):
        got(zres.at[i], z_recv.at[i])
        total = total + zres[i].astype(F32)
    gq_out[...] = total

    for copy in sends:
        copy.wait_send()
    for rd in range(4):
        for o in range(4):
            core_copy(rd, o).wait_send()


def hand_over(gq_in, gv_in, tg_in, gq_out, gv_out, tg_out):
    gq_out[...] = gq_in[...]
    gv_out[...] = gv_in[...]
    for i in range(3):
        tg_out[i] = tg_in[i, 0]


def on_device(queries, views, positives, query_weight, owners, view_weight, view_kinds, kind_scale):
    rows, width = queries.shape
    vcols = views.shape[0]
    nchunk = rows // CHUNK
    sub = rows // 64
    half = width // 2
    nrow = rows // 128
    pos = positives.reshape(nrow, 128)
    qw = query_weight.reshape(nrow, 128)
    own = owners.reshape(NPB, 1, vcols)
    vw = view_weight.reshape(NPB, 1, vcols)
    kind = view_kinds.reshape(NPB, 1, vcols)
    vmem = pl.BlockSpec(memory_space=pltpu.VMEM)
    V = pltpu.VMEM
    dma = pltpu.SemaphoreType.DMA
    gq, gv, tg = pl.pallas_call(
        functools.partial(kernel, rows * NPB),
        out_shape=(
            jax.ShapeDtypeStruct((sub, width), F32),
            jax.ShapeDtypeStruct((vcols, width), F32),
            jax.ShapeDtypeStruct((8, 128), F32),
        ),
        in_specs=[pl.BlockSpec(memory_space=pltpu.SMEM)] + [pl.BlockSpec(memory_space=pl.ANY)] * 7,
        out_specs=(vmem, vmem, vmem),
        scratch_shapes=[
            V((nrow, 128), jnp.int32),
            V((nrow, 128), F32),
            V((NPB, 1, vcols), jnp.int32),
            V((NPB, 1, vcols), F32),
            V((NPB, 1, vcols), jnp.int32),
            dma((6,)),
            V((rows, width), BF16),
            V((width, 2 * rows), BF16),
            V((2, 4, 4, 2, sub, width), BF16),
            V((2 * vcols, width), BF16),
            V((2 * rows, 2 * vcols), F32),
            V((2 * rows, 2 * vcols), BF16),
            V((2, sub, width), F32),
            V((2, sub, width), BF16),
            V((2 * nrow, 128), F32),
            V((2 * nrow, 128), F32),
            V((2 * rows, 128), F32),
            V((2 * rows, 128), F32),
            V((2 * rows, 128), F32),
            V((4, NY, NX, sub, width), F32),
            V((4, NY, NX, sub, width), F32),
            V((4, NY, NX, sub, width), F32),
            V((4, NX, NY, sub, half), BF16),
            V((4, NY, NX, sub, half), BF16),
            V((4, NX, NY, sub, half), BF16),
            V((4, NY, NX, sub, half), BF16),
            V((4, NY, sub, half), BF16),
            V((4, NX, sub, half), BF16),
            V((4, NY, sub, half), BF16),
            V((4, NX, sub, half), BF16),
            V((4, sub, width), F32),
            V((3, sub, width), BF16),
            V((3, sub, width), BF16),
            V((2, width, vcols), F32),
            V((width, vcols), BF16),
            V((width, vcols), BF16),
            V((2, 2 * nchunk, vcols), F32),
            V((3, nrow, 128), F32),
            V((2, 2, 1, vcols), F32),
            V((2, 1, vcols), F32),
            V((NA, 2, nrow, 128), F32),
            V((NB, 2, nrow, 128), F32),
            V((2, 2, nrow, 128), F32),
            V((2, nrow, 128), F32),
            V((NA, 8, 128), F32),
            V((NB, 8, 128), F32),
            V((2, 8, 128), F32),
            V((2, 8, 128), F32),
            dma((nchunk,)), dma((2,)),
            dma((40,)), dma((40,)),
            dma((8,)), dma((8,)),
            dma((4,)), dma((4,)),
            dma((2,)), dma((2,)),
            dma((NA + NB,)), dma((NA + NB,)),
            dma((NA + NB + 2,)), dma((NA + NB + 2,)),
            dma((16,)), dma((16,)),
            dma((64,)), dma((64,)),
            dma((4,)), dma((4,)),
        ],
        compiler_params=pltpu.CompilerParams(collective_id=0, has_side_effects=True,
                                             vmem_limit_bytes=63 * 1024 * 1024),
    )(kind_scale, views.reshape(2, 4, sub, width), queries.reshape(4, 4, 4, sub, width), pos, qw, own, vw, kind)
    smem = pl.BlockSpec(memory_space=pltpu.SMEM)
    return pl.pallas_call(
        hand_over,
        out_shape=(
            jax.ShapeDtypeStruct(gq.shape, F32),
            jax.ShapeDtypeStruct(gv.shape, F32),
            jax.ShapeDtypeStruct(kind_scale.shape, F32),
        ),
        in_specs=[vmem, vmem, smem],
        out_specs=(vmem, vmem, smem),
    )(gq, gv, tg)


def solution(mesh):
    in_specs = (P("pb", None), P(("vert", "pb"), None), P("pb"), P("pb"), P("vert"), P("vert"), P("vert"), P())
    out_specs = (P(("pb", "vert"), None), P(("vert", "pb"), None), P())
    return jax.shard_map(on_device, mesh=mesh, in_specs=in_specs, out_specs=out_specs, check_vma=False)
```

```python
import functools
import math

import jax
import jax.numpy as jnp
from jax import lax
from jax.experimental import pallas as pl
from jax.experimental.pallas import tpu as pltpu
from jax.sharding import PartitionSpec as P

MESH = pl.DeviceIdType.MESH
LOG2E = math.log2(math.e)
LN2 = math.log(2.0)
NPB = 4
NX = 4
NY = 4
NA = 8
NB = 8
CHUNK = 256
F32 = jnp.float32
BF16 = jnp.bfloat16


def kernel(total_queries, kscale_ref, views_hbm, q_hbm, pos_hbm, qw_hbm, own_hbm, vw_hbm, kind_hbm,
           gq_out, gv_out, tg_out,
           pos_ref, qw_ref, own_ref, vw_ref, kind_ref, in_sem,
           qb, qt, qf, vb, S, H, qslice, qzs, pq, pqf, rep, qwrep, posrep, gown, csend, crecv,
           sa1, sb1, ra1, rb1, sa2, sb2, ra2, rb2, res, zout, zres, gvt, zs, zr,
           colpart, rowpart, colx, colfin, rowa, rowb, rowc, rowfin, ta, tb, to, tp,
           qsem, slsem, ag_send, ag_recv, core_send, core_recv, vz_send, vz_recv,
           col_send, col_recv, row_send, row_recv, t_send, t_recv,
           c_send, c_recv, x_send, x_recv, z_send, z_recv):
    p = lax.axis_index("pb")
    v = lax.axis_index("vert")
    core = v % 2
    x = (v // 2) % NX
    y = (v // (2 * NX)) % NY
    zh = v // (2 * NX * NY)
    even = p % 2
    upper = p // 2
    mate = p + 1 - 2 * even
    far = (p + 2) % NPB
    a_me = zh * NX + x
    b_me = upper * NY + y
    rows, width = qb.shape
    nchunk = rows // CHUNK
    vcols = own_ref.shape[2]
    half = width // 2
    sub = gown.shape[3]

    def vert_of(zh_, y_, x_, c_):
        return ((zh_ * NY + y_) * NX + x_) * 2 + c_

    def remote(src, dst, ssem, rsem, dev):
        return pltpu.make_async_remote_copy(src_ref=src, dst_ref=dst, send_sem=ssem, recv_sem=rsem,
                                            device_id=dev, device_id_type=MESH)

    here = (p, v)
    sends = []

    def go(copy):
        copy.start()
        sends.append(copy)

    sl_a = (y * NX + x) * 2 + core
    sl_b = 8 * NY + (x * NY + y) * 2 + core
    slices = []
    for i, sl in enumerate((sl_a, sl_b)):
        slices.append(pltpu.make_async_copy(q_hbm.at[sl // 16, (sl // 4) % 4, sl % 4], qslice.at[i], slsem.at[i]))
        slices[-1].start()

    small = [pltpu.make_async_copy(src, dst, in_sem.at[i]) for i, (src, dst) in enumerate((
        (views_hbm, csend.at[0, pl.ds(0, 2)]), (pos_hbm, pos_ref), (qw_hbm, qw_ref), (own_hbm, own_ref), (vw_hbm, vw_ref),
        (kind_hbm, kind_ref)))]
    for copy in small:
        copy.start()

    def load(r):
        part = (r // 2, pl.ds((r % 2) * 2, 2))
        return pltpu.make_async_copy(q_hbm.at[part], gown.at[part], qsem.at[r])

    for r in range(nchunk):
        load(r).start()

    peers_a = []
    for d in range(1, NA):
        i = (a_me + d) % NA
        peers_a.append((p, vert_of(i // NX, y, i % NX, core)))
    peers_b = []
    for d in range(1, NB):
        i = (b_me + d) % NB
        peers_b.append(((i // NY) * 2 + even, vert_of(zh, i % NY, x, core)))
    over = (p, vert_of(1 - zh, y, x, core))
    far_over = (far, vert_of(1 - zh, y, x, core))
    twin = (p, vert_of(zh, y, x, 1 - core))
    peers = peers_a + peers_b + [twin, (mate, v), far_over]
    barrier = pltpu.get_barrier_semaphore()
    for dev in peers:
        pl.semaphore_signal(barrier, inc=1, device_id=dev, device_id_type=MESH)
    nrow = rows // 128
    for i in range(2):
        slices[i].wait()
        qzs[i] = qslice[i].astype(BF16)
    for copy in small:
        copy.wait()
    vb[0:vcols, :] = csend[0, 0:2].reshape(vcols, width).astype(BF16)
    pq[0:nrow, :] = pos_ref[...].astype(F32)
    pq[nrow:2 * nrow, :] = qw_ref[...]
    pl.semaphore_wait(barrier, len(peers))

    def to_far(i, src, dst):
        return remote(src, dst, vz_send.at[i], vz_recv.at[i], (far, v))

    go(to_far(0, qzs.at[0], qf.at[0, y, x, core]))
    go(to_far(1, qzs.at[1], qf.at[1, x, y, core]))
    views_copy = remote(vb.at[pl.ds(0, vcols)], vb.at[pl.ds(vcols, vcols)], vz_send.at[2], vz_recv.at[2], (mate, v))
    go(views_copy)
    go(to_far(3, pq, pqf))

    def to_x(d):
        return (p, vert_of(zh, y, (x + d) % NX, core))

    def to_y(d):
        return (p, vert_of(zh, (y + d) % NY, x, core))

    k0, k1, k2 = kscale_ref[0], kscale_ref[1], kscale_ref[2]
    blocks = (p, mate)

    def scale_of(k):
        kind = kind_ref[k]
        return jnp.where(kind == 0, k0, jnp.where(kind == 1, k1, k2))

    scales = [scale_of(k) for k in blocks]
    scales2 = [s * LOG2E for s in scales]

    def cast_queries(r, carry):
        load(r).wait()
        block = gown[r // 2, pl.ds((r % 2) * 2, 2)].reshape(CHUNK, width)
        at = pl.multiple_of(r * CHUNK, CHUNK)
        qb[pl.ds(at, CHUNK), :] = block.astype(BF16)
        return carry

    lax.fori_loop(0, nchunk, cast_queries, 0)

    def score(q, at, ch, slots, row_at):
        tiles = []
        for sl in slots:
            cols = slice(sl * vcols, (sl + 1) * vcols)
            s = lax.dot_general(q, vb[cols, :], (((1,), (1,)), ((), ())),
                                preferred_element_type=F32) * scales2[sl]
            S[pl.ds(at, CHUNK), cols] = s
            peak = jnp.max(s, axis=0, keepdims=True)
            colpart[sl, pl.ds(ch, 1), :] = peak + jnp.log2(jnp.sum(jnp.exp2(s - peak), axis=0, keepdims=True))
            tiles += [s[:, h * 128:(h + 1) * 128] for h in range(vcols // 128)]
        m = functools.reduce(jnp.maximum, tiles)
        total = functools.reduce(jnp.add, [jnp.exp2(t - m) for t in tiles])
        for i in range(CHUNK // 128):
            mt = m[i * 128:(i + 1) * 128, :].T
            lt = total[i * 128:(i + 1) * 128, :].T
            peak = jnp.max(mt, axis=0, keepdims=True)
            lse = peak + jnp.log2(jnp.sum(lt * jnp.exp2(mt - peak), axis=0, keepdims=True))
            rowpart[row_at[0], pl.ds(row_at[1] * 2 + i, 1), :] = lse

    def own_pass(sl, first, last):
        def step(i, carry):
            for j in range(2):
                r = i * 2 + j
                at = pl.multiple_of(r * CHUNK, CHUNK)
                score(qb[pl.ds(at, CHUNK), :], at, r, (sl,), (sl, r))
            return carry

        lax.fori_loop(first // 2, last // 2, step, 0)

    def far_pass(parts):
        for h, o in parts:
            r = h * 4 + o
            q = qf[h, o].reshape(CHUNK, width)
            at = pl.multiple_of(rows + r * CHUNK, CHUNK)
            score(q, at, r + nchunk, (0, 1), (2, r))

    def got(ref, sem):
        remote(ref, ref, sem, sem, here).wait_recv()

    def spread(src, first, dst, at0):
        for r in range(nrow):
            dst[at0 + r * 128:at0 + (r + 1) * 128, :] = jnp.broadcast_to(src[first + r:first + r + 1, :], (128, 128)).T

    def slice_a(i, dest, ssem, rsem):
        go(remote(qf.at[0, y, i, core], qf.at[0, y, i, core], ag_send.at[ssem], ag_recv.at[rsem], dest))

    def slice_b(i, dest, ssem, rsem):
        go(remote(qf.at[1, x, i, core], qf.at[1, x, i, core], ag_send.at[ssem], ag_recv.at[rsem], dest))

    def second_a(k):
        i = (x + k) % NX
        for d in (1, 3, 2):
            slice_a(i, to_y(d), 8 + k * 4 + d, 8 + y * 4 + i)

    def second_b(k):
        i = (y + k) % NY
        for d in (1, 3, 2):
            slice_b(i, to_x(d), 24 + k * 4 + d, 24 + x * 4 + i)

    own_pass(0, 0, 2)
    got(qf.at[0, y, x, core], vz_recv.at[0])
    for d in (1, 3, 2):
        slice_a(x, to_x(d), d, x)
    second_a(0)
    got(qf.at[1, x, y, core], vz_recv.at[1])
    for d in (1, 3, 2):
        slice_b(y, to_y(d), 4 + d, 4 + y)
    second_b(0)
    own_pass(0, 2, 8)
    for k in (1, 3, 2):
        got(qf.at[0, y, (x + k) % NX, core], ag_recv.at[(x + k) % NX])
        second_a(k)
        got(qf.at[1, x, (y + k) % NY, core], ag_recv.at[4 + (y + k) % NY])
        second_b(k)

    def to_twin(h, o):
        part = qf.at[h, o, :, core]
        go(remote(part, part, core_send.at[h * 4 + o], core_recv.at[h * 4 + o], twin))

    def from_twin(h, o):
        got(qf.at[h, o, :, 1 - core], core_recv.at[h * 4 + o])

    def arrive(d):
        o = (y + d) % NY
        for k in (0, 1, 3, 2):
            i = (x + k) % NX
            got(qf.at[0, o, i, core], ag_recv.at[8 + o * 4 + i])
        to_twin(0, o)
        o = (x + d) % NX
        for k in (0, 1, 3, 2):
            i = (y + k) % NY
            got(qf.at[1, o, i, core], ag_recv.at[24 + o * 4 + i])
        to_twin(1, o)

    def far_step(d):
        from_twin(0, (y + d) % NY)
        from_twin(1, (x + d) % NX)
        far_pass([(0, (y + d) % NY), (1, (x + d) % NX)])

    to_twin(0, y)
    to_twin(1, x)
    got(vb.at[pl.ds(vcols, vcols)], vz_recv.at[2])
    own_pass(1, 0, 8)
    far_step(0)
    got(pqf, vz_recv.at[3])
    arrive(1)
    arrive(3)
    far_step(1)
    arrive(2)
    far_step(3)
    far_step(2)

    def log_sum(parts):
        m = functools.reduce(jnp.maximum, parts)
        return m + jnp.log2(functools.reduce(jnp.add, [jnp.exp2(t - m) for t in parts]))

    def exchange_a(buf, ssem, rsem, base):
        for d in range(1, NA):
            go(remote(buf.at[a_me], buf.at[a_me], ssem.at[base + d], rsem.at[base + a_me], peers_a[d - 1]))

    def exchange_b(buf, ssem, rsem, base):
        for d in range(1, NB):
            go(remote(buf.at[b_me], buf.at[b_me], ssem.at[base + d], rsem.at[base + b_me], peers_b[d - 1]))

    def collect(buf, rsem, base, me, n):
        for d in range(1, n):
            src = (me + d) % n
            got(buf.at[src], rsem.at[base + src])

    rowc[0, upper] = log_sum([rowpart[0], rowpart[1]])
    rowc[0, 1 - upper] = rowpart[2]
    go(remote(rowc.at[0], rowc.at[1], col_send.at[1], col_recv.at[1], twin))
    for sl in range(2):
        part = colpart[sl]
        m = jnp.max(part, axis=0, keepdims=True)
        at = even if sl == 0 else 1 - even
        colx[even, at] = m + jnp.log2(jnp.sum(jnp.exp2(part - m), axis=0, keepdims=True))
    go(remote(colx.at[even], colx.at[even], col_send.at[0], col_recv.at[0], (mate, v)))
    got(rowc.at[1], col_recv.at[1])
    rowa[a_me] = log_sum([rowc[0], rowc[1]])
    exchange_a(rowa, row_send, row_recv, 0)

    def turn_own(i, carry):
        for j in range(2):
            at = pl.multiple_of((i * 2 + j) * CHUNK, CHUNK)
            qt[:, pl.ds(at, CHUNK)] = qb[pl.ds(at, CHUNK), :].T
        return carry

    def turn_far(i, carry):
        for j in range(2):
            r = i * 2 + j
            at = pl.multiple_of(rows + r * CHUNK, CHUNK)
            qt[:, pl.ds(at, CHUNK)] = qf[r // 4, r % 4].reshape(CHUNK, width).T
        return carry

    lax.fori_loop(0, nchunk // 2, turn_own, 0)
    spread(pqf, 0, posrep, rows)
    spread(pqf, nrow, qwrep, rows)
    collect(rowa, row_recv, 0, a_me, NA)
    rowb[b_me] = log_sum([rowa[i] for i in range(NA)])
    exchange_b(rowb, row_send, row_recv, NA)
    got(colx.at[1 - even], col_recv.at[0])
    for sl in range(2):
        at = even if sl == 0 else 1 - even
        colfin[sl] = log_sum([colx[0, at], colx[1, at]]) - jnp.log2(vw_ref[blocks[sl]])
    lax.fori_loop(0, nchunk // 2, turn_far, 0)
    spread(pq, 0, posrep, 0)
    spread(pq, nrow, qwrep, 0)
    collect(rowb, row_recv, NA, b_me, NB)
    rowfin[...] = log_sum([rowb[i] for i in range(NB)])
    pqw = (pq, pqf)
    for b in range(2):
        at = upper if b == 0 else 1 - upper
        rowpart[b] = rowfin[at] - jnp.log2(pqw[b][nrow:2 * nrow, :])

    def spread_lse(b):
        for r in range(nrow):
            rep[b * rows + r * 128:b * rows + (r + 1) * 128, :] = jnp.broadcast_to(rowpart[b, r:r + 1, :], (128, 128)).T

    spread_lse(1)

    lane = lax.broadcasted_iota(jnp.int32, (CHUNK, 128), 1).astype(F32)
    row_id = lax.broadcasted_iota(jnp.int32, (CHUNK, 128), 0)
    ntile = 2 * vcols // 128
    per = vcols // 128

    def tile(arr, h):
        return arr[h // per][:, (h % per) * 128:(h % per + 1) * 128]

    weights = [vw_ref[k] for k in blocks]
    owners = [own_ref[k] for k in blocks]
    shifts = [colfin[0], colfin[1]]
    col0 = [(v * (NPB * vcols) + k * vcols).astype(F32) for k in blocks]
    rounds = [(1, 1 - zh), (0, 1 - zh), (1, zh), (0, zh)]

    def core_copy(rd, o):
        return remote(csend.at[rd, o], crecv.at[rd, o], c_send.at[rd * 4 + o], c_recv.at[rd * 4 + o], twin)

    def grad_step(rd, o, terms):
        b, z = rounds[rd]
        at = pl.multiple_of(b * rows + z * (rows // 2) + o * CHUNK, CHUNK)
        first_row = (p if b == 0 else far) * rows + z * (rows // 2) + o * CHUNK
        ra, rw, rp = rep[pl.ds(at, CHUNK), :], qwrep[pl.ds(at, CHUNK), :], posrep[pl.ds(at, CHUNK), :]
        out, pieces = [], []
        for h in range(ntile):
            s = S[pl.ds(at, CHUNK), h * 128:(h + 1) * 128]
            g = jnp.exp2(s - ra) + jnp.exp2(s - tile(shifts, h))
            col = lane + (col0[h // per] + (h % per) * 128)
            g = g - jnp.where(rp == col, rw, 0.0)
            g = g - jnp.where(row_id == tile(owners, h) - first_row, tile(weights, h), 0.0)
            pieces.append((g * tile(scales, h)).astype(BF16))
            out.append(terms[h] + jnp.sum(g * s, axis=0, keepdims=True))
        hh = jnp.concatenate(pieces, axis=1)
        H[pl.ds(at, CHUNK), :] = hh
        acc = jnp.dot(hh, vb[...], preferred_element_type=F32).reshape(NX, 2, sub, width)
        first, second = acc[:, 0], acc[:, 1]
        gown[rd, o] = jnp.where(core == 0, first, second)
        csend[rd, o] = jnp.where(core == 0, second, first)
        core_copy(rd, o).start()
        return tuple(out)

    def grad_half(rd, part, terms):
        for j in range(2):
            terms = grad_step(rd, part * 2 + j, terms)
        return terms

    def fold_core(rd):
        def step(o, carry):
            core_copy(rd, o).wait_recv()
            for i in range(NX):
                val = gown[rd, o, i] + crecv[rd, o, i]
                gown[rd, o, i] = val
                sa1[rd, i, o] = val[:, :half].astype(BF16)
                sb1[rd, o, i] = val[:, half:].astype(BF16)
            return carry

        lax.fori_loop(0, NY, step, 0)
        for d in (1, 3, 2):
            go(remote(sa1.at[rd, (x + d) % NX], ra1.at[rd, x], x_send.at[rd * 16 + d], x_recv.at[rd * 16 + x], to_x(d)))
            go(remote(sb1.at[rd, (y + d) % NY], rb1.at[rd, y], x_send.at[rd * 16 + 4 + d], x_recv.at[rd * 16 + 4 + y],
                      to_y(d)))

    def fold_first(rd):
        for d in (1, 3, 2):
            got(ra1.at[rd, (x + d) % NX], x_recv.at[rd * 16 + (x + d) % NX])
        for o in range(NY):
            val = gown[rd, o, x][:, :half]
            for d in range(1, NX):
                val = val + ra1[rd, (x + d) % NX, o].astype(F32)
            gown[rd, o, x, :, 0:half] = val
            sa2[rd, o] = val.astype(BF16)
        for d in (1, 3, 2):
            go(remote(sa2.at[rd, (y + d) % NY], ra2.at[rd, y], x_send.at[rd * 16 + 8 + d], x_recv.at[rd * 16 + 8 + y],
                      to_y(d)))
        for d in (1, 3, 2):
            got(rb1.at[rd, (y + d) % NY], x_recv.at[rd * 16 + 4 + (y + d) % NY])
        for i in range(NX):
            val = gown[rd, y, i][:, half:]
            for d in range(1, NY):
                val = val + rb1[rd, (y + d) % NY, i].astype(F32)
            gown[rd, y, i, :, half:width] = val
            sb2[rd, i] = val.astype(BF16)
        for d in (1, 3, 2):
            go(remote(sb2.at[rd, (x + d) % NX], rb2.at[rd, x], x_send.at[rd * 16 + 12 + d],
                      x_recv.at[rd * 16 + 12 + x], to_x(d)))

    def fold_second(rd):
        for d in (1, 3, 2):
            got(ra2.at[rd, (y + d) % NY], x_recv.at[rd * 16 + 8 + (y + d) % NY])
        val = gown[rd, y, x, :, 0:half]
        for d in range(1, NY):
            val = val + ra2[rd, (y + d) % NY].astype(F32)
        res[rd, :, :half] = val
        for d in (1, 3, 2):
            got(rb2.at[rd, (x + d) % NX], x_recv.at[rd * 16 + 12 + (x + d) % NX])
        val = gown[rd, y, x, :, half:width]
        for d in range(1, NX):
            val = val + rb2[rd, (x + d) % NX].astype(F32)
        res[rd, :, half:] = val
        if rd < 3:
            zout[rd] = res[rd].astype(BF16)
            go(remote(zout.at[rd], zres.at[rd], z_send.at[rd], z_recv.at[rd], (far_over, over, (far, v))[rd]))

    def grad_views(sl):
        def step(i, carry):
            at = pl.multiple_of(i * CHUNK, CHUNK)
            gvt[sl, pl.ds(at, CHUNK), :] = jnp.dot(qt[pl.ds(at, CHUNK), :], H[:, sl * vcols:(sl + 1) * vcols],
                                                   preferred_element_type=F32)
            return carry

        lax.fori_loop(0, width // CHUNK, step, 0)

    terms = (jnp.zeros((1, 128), F32),) * ntile
    terms = grad_half(0, 0, terms)
    terms = grad_half(0, 1, terms)
    spread_lse(0)
    fold_core(0)
    terms = grad_half(1, 0, terms)
    terms = grad_half(1, 1, terms)
    terms = grad_half(2, 0, terms)
    fold_core(1)
    terms = grad_half(2, 1, terms)
    terms = grad_half(3, 0, terms)
    fold_core(2)
    fold_first(0)
    terms = grad_half(3, 1, terms)

    kinds = []
    for t in range(3):
        kinds.append(functools.reduce(jnp.add, [
            jnp.where(tile([kind_ref[k] for k in blocks], h) == t, terms[h], 0.0) for h in range(ntile)]))
    to[0] = jnp.concatenate(kinds + [jnp.zeros((5, 128), F32)], axis=0) * (LN2 / total_queries)
    go(remote(to.at[0], to.at[1], t_send.at[NA + NB], t_recv.at[NA + NB], twin))
    got(to.at[1], t_recv.at[NA + NB])
    ta[a_me] = to[0] + to[1]
    exchange_a(ta, t_send, t_recv, 0)
    fold_core(3)
    fold_second(0)
    grad_views(1)
    zs[...] = gvt[1].astype(BF16)
    go(remote(zs, zr, z_send.at[3], z_recv.at[3], (mate, v)))
    fold_first(1)
    collect(ta, t_recv, 0, a_me, NA)
    tb[b_me] = functools.reduce(jnp.add, [ta[i] for i in range(NA)])
    exchange_b(tb, t_send, t_recv, NA)
    grad_views(0)
    fold_first(2)
    fold_second(1)
    collect(tb, t_recv, NA, b_me, NB)
    tp[0] = functools.reduce(jnp.add, [tb[i] for i in range(NB)])
    go(remote(tp.at[0], tp.at[1], t_send.at[NA + NB + 1], t_recv.at[NA + NB + 1], (mate, v)))
    fold_first(3)
    fold_second(2)
    got(zr, z_recv.at[3])
    gv_out[...] = (gvt[0] + zr[...].astype(F32)).T
    got(tp.at[1], t_recv.at[NA + NB + 1])
    sums = jnp.sum(tp[0] + tp[1], axis=1, keepdims=True)
    tg_out[...] = jnp.broadcast_to(sums, tg_out.shape)
    fold_second(3)
    total = res[3]
    for i in range(3):
        got(zres.at[i], z_recv.at[i])
        total = total + zres[i].astype(F32)
    gq_out[...] = total

    for copy in sends:
        copy.wait_send()
    for rd in range(4):
        for o in range(4):
            core_copy(rd, o).wait_send()


def hand_over(gq_in, gv_in, tg_in, gq_out, gv_out, tg_out):
    gq_out[...] = gq_in[...]
    gv_out[...] = gv_in[...]
    for i in range(3):
        tg_out[i] = tg_in[i, 0]


def on_device(queries, views, positives, query_weight, owners, view_weight, view_kinds, kind_scale):
    rows, width = queries.shape
    vcols = views.shape[0]
    nchunk = rows // CHUNK
    sub = rows // 64
    half = width // 2
    nrow = rows // 128
    pos = positives.reshape(nrow, 128)
    qw = query_weight.reshape(nrow, 128)
    own = owners.reshape(NPB, 1, vcols)
    vw = view_weight.reshape(NPB, 1, vcols)
    kind = view_kinds.reshape(NPB, 1, vcols)
    vmem = pl.BlockSpec(memory_space=pltpu.VMEM)
    V = pltpu.VMEM
    dma = pltpu.SemaphoreType.DMA
    gq, gv, tg = pl.pallas_call(
        functools.partial(kernel, rows * NPB),
        out_shape=(
            jax.ShapeDtypeStruct((sub, width), F32),
            jax.ShapeDtypeStruct((vcols, width), F32),
            jax.ShapeDtypeStruct((8, 128), F32),
        ),
        in_specs=[pl.BlockSpec(memory_space=pltpu.SMEM)] + [pl.BlockSpec(memory_space=pl.ANY)] * 7,
        out_specs=(vmem, vmem, vmem),
        scratch_shapes=[
            V((nrow, 128), jnp.int32),
            V((nrow, 128), F32),
            V((NPB, 1, vcols), jnp.int32),
            V((NPB, 1, vcols), F32),
            V((NPB, 1, vcols), jnp.int32),
            dma((6,)),
            V((rows, width), BF16),
            V((width, 2 * rows), BF16),
            V((2, 4, 4, 2, sub, width), BF16),
            V((2 * vcols, width), BF16),
            V((2 * rows, 2 * vcols), F32),
            V((2 * rows, 2 * vcols), BF16),
            V((2, sub, width), F32),
            V((2, sub, width), BF16),
            V((2 * nrow, 128), F32),
            V((2 * nrow, 128), F32),
            V((2 * rows, 128), F32),
            V((2 * rows, 128), F32),
            V((2 * rows, 128), F32),
            V((4, NY, NX, sub, width), F32),
            V((4, NY, NX, sub, width), F32),
            V((4, NY, NX, sub, width), F32),
            V((4, NX, NY, sub, half), BF16),
            V((4, NY, NX, sub, half), BF16),
            V((4, NX, NY, sub, half), BF16),
            V((4, NY, NX, sub, half), BF16),
            V((4, NY, sub, half), BF16),
            V((4, NX, sub, half), BF16),
            V((4, NY, sub, half), BF16),
            V((4, NX, sub, half), BF16),
            V((4, sub, width), F32),
            V((3, sub, width), BF16),
            V((3, sub, width), BF16),
            V((2, width, vcols), F32),
            V((width, vcols), BF16),
            V((width, vcols), BF16),
            V((2, 2 * nchunk, vcols), F32),
            V((3, nrow, 128), F32),
            V((2, 2, 1, vcols), F32),
            V((2, 1, vcols), F32),
            V((NA, 2, nrow, 128), F32),
            V((NB, 2, nrow, 128), F32),
            V((2, 2, nrow, 128), F32),
            V((2, nrow, 128), F32),
            V((NA, 8, 128), F32),
            V((NB, 8, 128), F32),
            V((2, 8, 128), F32),
            V((2, 8, 128), F32),
            dma((nchunk,)), dma((2,)),
            dma((40,)), dma((40,)),
            dma((8,)), dma((8,)),
            dma((4,)), dma((4,)),
            dma((2,)), dma((2,)),
            dma((NA + NB,)), dma((NA + NB,)),
            dma((NA + NB + 2,)), dma((NA + NB + 2,)),
            dma((16,)), dma((16,)),
            dma((64,)), dma((64,)),
            dma((4,)), dma((4,)),
        ],
        compiler_params=pltpu.CompilerParams(collective_id=0, has_side_effects=True,
                                             vmem_limit_bytes=63 * 1024 * 1024),
    )(kind_scale, views.reshape(2, 4, sub, width), queries.reshape(4, 4, 4, sub, width), pos, qw, own, vw, kind)
    smem = pl.BlockSpec(memory_space=pltpu.SMEM)
    return pl.pallas_call(
        hand_over,
        out_shape=(
            jax.ShapeDtypeStruct(gq.shape, F32),
            jax.ShapeDtypeStruct(gv.shape, F32),
            jax.ShapeDtypeStruct(kind_scale.shape, F32),
        ),
        in_specs=[vmem, vmem, smem],
        out_specs=(vmem, vmem, smem),
    )(gq, gv, tg)


def solution(mesh):
    in_specs = (P("pb", None), P(("vert", "pb"), None), P("pb"), P("pb"), P("vert"), P("vert"), P("vert"), P())
    out_specs = (P(("pb", "vert"), None), P(("vert", "pb"), None), P())
    return jax.shard_map(on_device, mesh=mesh, in_specs=in_specs, out_specs=out_specs, check_vma=False)
```
